256 devices in a mesh: pipe: 4 (over y), dp: 4 (over x), tensor: 16 (over z, core).
Axes of the slice: x: 4, y: 4, z: 8, core: 2. Of those that a mesh axis runs over, the one named last changes fastest.
Arguments:
- tokens: bfloat16 [4, 2048, 3072], P('pipe', 'dp', 'tensor'), may hold values from -6 to 6
- cotangent: bfloat16 [4, 2048, 3072], P('pipe', 'dp', 'tensor'), may hold values from -6 to 6
- w_in: bfloat16 [4, 3072, 12288], P('pipe', None, 'tensor'), may hold values from -0.109375 to 0.109375
- w_out: bfloat16 [4, 12288, 3072], P('pipe', 'tensor'), may hold values from -0.0546875 to 0.0546875
- levels: int32 [4, 16], P('pipe', 'dp'), may hold values from 1 to 16
Outputs:
- received: bfloat16 [4, 2048, 3072], P('pipe', 'dp', 'tensor')
- grad_in: bfloat16 [4, 3072, 12288], P('pipe', 'dp', 'tensor')
- grad_out: bfloat16 [4, 12288, 3072], P('pipe', 'tensor', 'dp')
The draws below stay inside these ranges and needn't reach their ends.
All inputs are finite; a program needn't handle non-finite values.
Results may differ from the reference program's by a relative error of at most 0.02.
Values may be sent and summed in bfloat16 or wider, within the bound.
No kernel may reach another device: no remote copies, remote signals or barrier semaphores. Data moves between devices by JAX's collectives and lax.ppermute only.
A program may use at most 128 MiB of HBM per device.

```python
import math
import jax
import jax.numpy as jnp
from jax import lax

D = 3072
FF = 12288
BLOCK = 128
TOK_DEV = 512
TOKENS = 2048
SECTIONS = 4
SHARDS = 16
N_DP = 4
N_TENSOR = 16


def touch_ends(entries, stream_key, smallest, largest):
    longest = entries.shape.index(max(entries.shape))
    spots = []
    for shift in (0, 1):
        where = [jax.random.randint(jax.random.fold_in(stream_key, axis), (), 0, length) for axis, length in enumerate(entries.shape)]
        where[longest] = (where[longest] + shift) % entries.shape[longest]
        spots.append(tuple(where))
    return entries.at[spots[0]].set(smallest).at[spots[1]].set(largest)


def level_of(key, extent, cuts, smallest, largest):
    level = 1.0
    for position, parts in cuts:
        draws = jax.random.uniform(jax.random.fold_in(jax.random.fold_in(key, 6), position), (parts,), jnp.float32, smallest / len(cuts), largest / len(cuts))
        level = level * jnp.repeat(jnp.exp(draws), extent[position] // parts).reshape((-1,) + (1,) * (len(extent) - 1 - position))
    return level


def scatter_about(stream_key, dims, deviation, most, pieces=(), kind=jnp.bfloat16):
    drawn = deviation * jax.random.normal(stream_key, dims, jnp.float32)
    if pieces:
        drawn = drawn * level_of(stream_key, dims, pieces, -0.22, 0.18)
    return jnp.clip(drawn, -most, most).astype(kind)


def setup_inputs(seed: int = 0) -> dict:
    splits = jax.random.split(jax.random.key(seed), 6)
    return {
        "tokens": scatter_about(splits[0], (SECTIONS, TOKENS, D), 1.0, 6.0, ((0, 4), (1, 4), (2, 16))),
        "cotangent": scatter_about(splits[1], (SECTIONS, TOKENS, D), 1.0, 6.0, ((0, 4), (1, 4), (2, 16))),
        "w_in": scatter_about(splits[2], (SECTIONS, D, FF), D ** -0.5, 0.109375, ((0, 4), (2, 16))),
        "w_out": scatter_about(splits[3], (SECTIONS, FF, D), FF ** -0.5, 0.0546875, ((0, 4), (1, 16))),
        "levels": touch_ends(jax.random.randint(splits[4], (SECTIONS, TOKENS // BLOCK), 1, SHARDS + 1), jax.random.fold_in(splits[4], 1), 1, SHARDS).astype(jnp.int32),
    }


def section_grads(tok_rows, cot_rows, weight_in, weight_out, width_levels):
    shard_width = FF // N_TENSOR
    column_shard = jnp.arange(FF, dtype=jnp.int32) // shard_width
    token_level = jnp.repeat(width_levels, BLOCK)
    keep_mask = (column_shard[None, :] < token_level[:, None]).astype(jnp.float32)
    preact = jnp.dot(tok_rows, weight_in, preferred_element_type=jnp.float32)
    rectified = jnp.maximum(preact, 0.0)
    squared = (rectified * rectified * keep_mask).astype(jnp.bfloat16)
    act_grad = jnp.dot(cot_rows, weight_out.T, preferred_element_type=jnp.float32)
    hid_grad = (act_grad * 2.0 * rectified * keep_mask).astype(jnp.bfloat16)
    input_grad = jnp.dot(hid_grad, weight_in.T, preferred_element_type=jnp.float32).astype(jnp.bfloat16)
    summed_in = jnp.zeros((D, FF), jnp.float32)
    summed_out = jnp.zeros((FF, D), jnp.float32)
    for group in range(N_DP):
        lower = group * TOK_DEV
        part_in = jnp.dot(tok_rows[lower:lower + TOK_DEV].T, hid_grad[lower:lower + TOK_DEV], preferred_element_type=jnp.float32).astype(jnp.bfloat16)
        part_out = jnp.dot(squared[lower:lower + TOK_DEV].T, cot_rows[lower:lower + TOK_DEV], preferred_element_type=jnp.float32).astype(jnp.bfloat16)
        part_in, part_out = lax.optimization_barrier((part_in, part_out))
        summed_in = summed_in + part_in.astype(jnp.float32)
        summed_out = summed_out + part_out.astype(jnp.float32)
    grad_scale = 1.0 / math.sqrt(TOKENS)
    return (input_grad, (summed_in * grad_scale).astype(jnp.bfloat16), (summed_out * grad_scale).astype(jnp.bfloat16))

def reference(tokens, cotangent, w_in, w_out, levels):
    inputs_all = []
    grads_in = []
    grads_out = []
    for section in range(SECTIONS):
        input_grad, grad_first, grad_second = section_grads(tokens[section], cotangent[section], w_in[section], w_out[section], levels[section])
        inputs_all.append(input_grad)
        grads_in.append(grad_first)
        grads_out.append(grad_second)
    received = jnp.stack(inputs_all[1:] + [jnp.zeros_like(inputs_all[0])])
    return (received, jnp.stack(grads_in), jnp.stack(grads_out))
```

```python
import math

import jax
import jax.numpy as jnp
from jax import lax
from jax.experimental import pallas as pl
from jax.experimental.pallas import tpu as pltpu
from jax.sharding import Mesh
from jax.sharding import PartitionSpec as P

BLOCK = 128
MIB = 1 << 20
F32 = jnp.float32
BF16 = jnp.bfloat16
VMEM = pl.BlockSpec(memory_space=pltpu.VMEM)
SMEM = pl.BlockSpec(memory_space=pltpu.SMEM)
NN = (((1,), (0,)), ((), ()))
NT = (((1,), (1,)), ((), ()))
TN = (((0,), (0,)), ((), ()))


def shift(block, axis, distance):
    n = lax.axis_size(axis)
    return lax.ppermute(block, axis, [(i, (i + distance) % n) for i in range(n)])


def dot(left, right, dims):
    return lax.dot_general(left, right, dims, preferred_element_type=F32)


def params(mib=48):
    return pltpu.CompilerParams(vmem_limit_bytes=mib * MIB)


def cost(flops, nbytes):
    return pl.CostEstimate(flops=flops, bytes_accessed=nbytes, transcendentals=0)


def ring_gather(piece):
    half = piece.shape[0] // 2
    l1, r1 = shift(piece, "z", 1), shift(piece, "z", -1)
    l2, r2 = shift(l1, "z", 1), shift(r1, "z", -1)
    near = jnp.concatenate([piece, l1, r1, l2, r2])
    l3, r3 = shift(l2, "z", 1), shift(r2, "z", -1)
    l4, r4 = shift(l3[:half], "z", 1), shift(r3[half:], "z", -1)
    far = jnp.concatenate([l3, r3, l4, r4])
    return near, far, shift(near, "core", 1), shift(far, "core", 1)


NEAR, FAR = (0, -1, 1, -2, 2), (-3, 3, 4)


def lay_out(pos_ref, tile, near, far, near_other, far_other):
    z, core = pos_ref[0], pos_ref[1]
    height = near.shape[0] // len(NEAR)
    for offsets, own, other in ((NEAR, near, near_other), (FAR, far, far_other)):
        for n, k in enumerate(offsets):
            base = lax.rem(z + (k + 8), 8) * (2 * height)
            rows = pl.ds(n * height, height)
            tile[pl.ds(pl.multiple_of(base + core * height, 64), height), :] = own[rows, :]
            tile[pl.ds(pl.multiple_of(base + (1 - core) * height, 64), height), :] = other[rows, :]


def hand_out(pos_ref, tile, own_ref, send_ref):
    dp, rank = pos_ref[2], pos_ref[0] * 2 + pos_ref[1]
    rows, share = own_ref.shape[0], send_ref.shape[1]
    own_ref[...] = tile[pl.ds(pl.multiple_of(dp * rows, 64), rows), :]
    for d in (1, 2, 3):
        first = lax.rem(dp + d, 4) * rows + rank * share
        send_ref[d - 1] = tile[pl.ds(pl.multiple_of(first, 16), share), :]


def keep_row(pos_ref, levels_ref, tokens):
    rank = pos_ref[0] * 2 + pos_ref[1]
    return jnp.concatenate(
        [
            jnp.full((1, BLOCK), (levels_ref[b] > rank).astype(F32), F32)
            for b in range(tokens // BLOCK)
        ],
        axis=1,
    )


def up_kernel(pos_ref, levels_ref, near, far, near_o, far_o, w_ref, rect_ref, sq_ref, own_ref, send_ref, tile):
    lay_out(pos_ref, tile, near, far, near_o, far_o)
    hand_out(pos_ref, tile, own_ref, send_ref)
    keep = keep_row(pos_ref, levels_ref, tile.shape[1])
    rect = jnp.maximum(dot(w_ref[...], tile[...], TN), 0.0)
    rect_ref[...] = rect
    sq_ref[...] = (rect * rect * keep).astype(BF16)


def down_kernel(pos_ref, levels_ref, near, far, near_o, far_o, w_ref, rect_ref, hid_ref, own_ref, send_ref, tile):
    lay_out(pos_ref, tile, near, far, near_o, far_o)
    hand_out(pos_ref, tile, own_ref, send_ref)
    keep = keep_row(pos_ref, levels_ref, tile.shape[1])
    grad = dot(w_ref[...], tile[...], NN)
    hid_ref[...] = (grad * 2.0 * rect_ref[...] * keep).astype(BF16)


def back_kernel(pos_ref, w_ref, w_other_ref, hid_ref, hid_other_ref, out_ref):
    z, core = pos_ref[0], pos_ref[1]
    height = out_ref.shape[1]
    for k in range(8):
        chip = lax.rem(z + k, 8)
        rows = pl.ds(pl.multiple_of(chip * (2 * height) + core * height, 64), height)
        term = dot(w_ref[rows, :], hid_ref[...], NN) + dot(w_other_ref[chip], hid_other_ref[...], NN)
        out_ref[k] = term.astype(BF16)


def wgrad_kernel(scale, flip, blk_own, blk_rest, h_own, h_l, h_r, h_o1, h_o2, out_ref):
    t = h_own.shape[1]
    h_o = jnp.concatenate([h_o1[...], h_o2[...]], axis=0)
    acc = None
    for n, (h, blk) in enumerate(
        ((h_own[...], blk_own[...]), (h_l[...], blk_rest[:, :t]), (h_r[...], blk_rest[:, t : 2 * t]), (h_o, blk_rest[:, 2 * t :]))
    ):
        term = dot(h, blk, NT) if flip else dot(blk, h, NT)
        acc = term if acc is None else acc + term
    out_ref[...] = (acc * scale).astype(BF16)


def dp_gather(block):
    half = block.shape[0] // 2
    left, right = shift(block, "dp", 1), shift(block, "dp", -1)
    return left, right, shift(left[:half], "dp", 1), shift(right[half:], "dp", -1)


def spread(send):
    rows = jnp.concatenate(
        [shift(send[0], "dp", 1), shift(send[2], "dp", -1), shift(send[1], "dp", 2)], axis=1
    )
    return lax.all_gather(rows, ("z", "core"), axis=0, tiled=True)


def ring_scatter(blocks):
    half = blocks.shape[1] // 2

    def plus(a, b):
        return (a.astype(F32) + b.astype(F32)).astype(BF16)

    right = shift(blocks[4, :half], "z", 1)
    left = shift(blocks[4, half:], "z", -1)
    right = shift(jnp.concatenate([plus(blocks[3, :half], right), blocks[3, half:]]), "z", 1)
    left = shift(jnp.concatenate([blocks[5, :half], plus(blocks[5, half:], left)]), "z", -1)
    right = shift(plus(blocks[2], right), "z", 1)
    left = shift(plus(blocks[6], left), "z", -1)
    right = shift(plus(blocks[1], right), "z", 1)
    left = shift(plus(blocks[7], left), "z", -1)
    return (blocks[0].astype(F32) + right.astype(F32) + left.astype(F32)).astype(BF16)


def shards(tokens, cotangent, w_in, w_out, levels):
    z, core, dp = lax.axis_index("z"), lax.axis_index("core"), lax.axis_index("dp")
    pos = jnp.stack([z, core, dp]).astype(jnp.int32)
    w_in, w_out, levels = w_in[0], w_out[0], levels[0]
    d, f = w_in.shape
    t, width = tokens.shape[1:]
    rows = d // 4
    share = rows // 16
    flops = 2 * t * d * f

    tok = ring_gather(tokens[0].T)
    cot = ring_gather(cotangent[0].T)
    w_split = w_in.reshape(8, 2, width, f)
    w_other = shift(lax.dynamic_index_in_dim(w_split, 1 - core, 1, False), "core", 1)

    tile = [pltpu.VMEM((d, t), BF16)]
    side = (jax.ShapeDtypeStruct((rows, t), BF16), jax.ShapeDtypeStruct((3, share, t), BF16))
    rect, sq, tok_own, tok_send = pl.pallas_call(
        up_kernel,
        out_shape=(jax.ShapeDtypeStruct((f, t), F32), jax.ShapeDtypeStruct((f, t), BF16)) + side,
        in_specs=[SMEM, SMEM] + [VMEM] * 5,
        out_specs=[VMEM] * 4,
        scratch_shapes=tile,
        compiler_params=params(),
        cost_estimate=cost(flops, 12 * MIB),
        name="up",
    )(pos, levels, *tok, w_in)
    sq_all = dp_gather(sq)
    tok_rest = spread(tok_send)
    hid, cot_own, cot_send = pl.pallas_call(
        down_kernel,
        out_shape=(jax.ShapeDtypeStruct((f, t), BF16),) + side,
        in_specs=[SMEM, SMEM] + [VMEM] * 6,
        out_specs=[VMEM] * 3,
        scratch_shapes=tile,
        compiler_params=params(),
        cost_estimate=cost(flops, 12 * MIB),
        name="down",
    )(pos, levels, *cot, w_out, rect)
    hid_other = shift(hid, "core", 1)
    hid_all = dp_gather(hid)
    cot_rest = spread(cot_send)
    terms = pl.pallas_call(
        back_kernel,
        out_shape=jax.ShapeDtypeStruct((8, width, t), BF16),
        in_specs=[SMEM] + [VMEM] * 4,
        out_specs=VMEM,
        compiler_params=params(),
        cost_estimate=cost(flops, 10 * MIB),
        name="back",
    )(pos, w_in, w_other, hid, hid_other)
    input_sum = ring_scatter(terms)
    n_pipe = lax.axis_size("pipe")
    received = lax.ppermute(input_sum, "pipe", [(i, i - 1) for i in range(1, n_pipe)])

    scale = 1.0 / math.sqrt(t * lax.axis_size("dp"))

    def wgrad(flip, own, rest, h_own, h_all, name):
        def kernel(*refs):
            wgrad_kernel(scale, flip, *refs)

        return pl.pallas_call(
            kernel,
            out_shape=jax.ShapeDtypeStruct((f, rows) if flip else (rows, f), BF16),
            in_specs=[VMEM] * 7,
            out_specs=VMEM,
            compiler_params=params(),
            cost_estimate=cost(flops, 8 * MIB),
            name=name,
        )(own, rest, h_own, *h_all)

    grad_out = wgrad(True, cot_own, cot_rest, sq, sq_all, "grad_out")
    grad_in = wgrad(False, tok_own, tok_rest, hid, hid_all, "grad_in")
    return (received.T[None], grad_in[None], grad_out[None])


def solution(mesh):
    n_pipe, n_dp, n_tensor = mesh.devices.shape
    fine = Mesh(mesh.devices.reshape(n_pipe, n_dp, n_tensor // 2, 2), ("pipe", "dp", "z", "core"))
    tensor = ("z", "core")
    return jax.shard_map(
        shards,
        mesh=fine,
        in_specs=(
            P("pipe", "dp", tensor),
            P("pipe", "dp", tensor),
            P("pipe", None, tensor),
            P("pipe", tensor, None),
            P("pipe", "dp"),
        ),
        out_specs=(P("pipe", "dp", tensor), P("pipe", "dp", tensor), P("pipe", tensor, "dp")),
        check_vma=False,
    )
```

```python
import functools
import math

import jax
import jax.numpy as jnp
from jax import lax
from jax.experimental import pallas as pl
from jax.experimental.pallas import tpu as pltpu
from jax.sharding import Mesh
from jax.sharding import PartitionSpec as P

BLOCK = 128
MIB = 1 << 20
F32 = jnp.float32
BF16 = jnp.bfloat16
VMEM = pl.BlockSpec(memory_space=pltpu.VMEM)
SMEM = pl.BlockSpec(memory_space=pltpu.SMEM)
NN = (((1,), (0,)), ((), ()))
NT = (((1,), (1,)), ((), ()))
TN = (((0,), (0,)), ((), ()))


def shift(block, axis, distance):
    n = lax.axis_size(axis)
    return lax.ppermute(block, axis, [(i, (i + distance) % n) for i in range(n)])


def dot(left, right, dims):
    return lax.dot_general(left, right, dims, preferred_element_type=F32)


def after(block, *done):
    return lax.optimization_barrier((block, *done))[0]


def both(left, right, axis):
    return shift(left, axis, 1), shift(right, axis, -1)


def params(mib=14):
    return pltpu.CompilerParams(vmem_limit_bytes=mib * MIB)


def cost(flops, nbytes):
    return pl.CostEstimate(flops=flops, bytes_accessed=nbytes, transcendentals=0)


def sds(*shape, dtype=BF16):
    return jax.ShapeDtypeStruct(shape, dtype)


OFFSETS = (0, -1, 1, -2, 2, -3, 3, 4)


def ring_gather(piece):
    half = piece.shape[0] // 2
    l1, r1 = both(piece, piece, "z")
    l2, r2 = both(l1, r1, "z")
    l3, r3 = both(l2, r2, "z")
    l4, r4 = both(l3[:half], r3[half:], "z")
    return piece, l1, r1, l2, r2, l3, r3, l4, r4


def column_kernel(pos_ref, *refs):
    *pieces, out_ref = refs
    half = out_ref.shape[1] // 2
    for k, piece in zip(OFFSETS, pieces):
        chip = lax.rem(pos_ref[0] + (k + 8), 8)
        if k == 4:
            out_ref[chip, :half] = piece[...]
            out_ref[chip, half:] = pieces[-1][...]
        else:
            out_ref[chip] = piece[...]


def column(pos, pieces, name):
    height, width = pieces[0].shape
    return pl.pallas_call(
        column_kernel,
        out_shape=sds(8, height, width),
        in_specs=[SMEM] + [VMEM] * len(pieces),
        out_specs=VMEM,
        compiler_params=params(),
        cost_estimate=cost(0, 2 * 16 * height * width),
        name=name,
    )(pos, *pieces)


def lay_out(pos_ref, tile, own, other):
    core = pos_ref[1]
    height = own.shape[1]
    for chip in range(8):
        base = chip * 2 * height
        tile[pl.ds(pl.multiple_of(base + core * height, 64), height), :] = own[chip]
        tile[pl.ds(pl.multiple_of(base + (1 - core) * height, 64), height), :] = other[chip]


def hand_out(pos_ref, tile, own_ref, sends, base, share):
    dp, rank = pos_ref[2], pos_ref[0] * 2 + pos_ref[1]
    rows = own_ref.shape[0]
    own_ref[...] = tile[pl.ds(pl.multiple_of(dp * rows, 64), rows), :]
    for d, send in zip((1, 2, 3), sends):
        first = lax.rem(dp + d, 4) * rows + rank * share
        send[base : base + share, :] = tile[pl.ds(pl.multiple_of(first, 16), share), :]


def keep_row(pos_ref, levels_ref, tokens):
    rank = pos_ref[0] * 2 + pos_ref[1]
    return jnp.concatenate(
        [
            jnp.full((1, BLOCK), (levels_ref[b] > rank).astype(F32), F32)
            for b in range(tokens // BLOCK)
        ],
        axis=1,
    )


def up_kernel(share, pos_ref, levels_ref, own, other, w_ref, rect_ref, sq_ref, blk_ref, s1, s2, s3, tile):
    lay_out(pos_ref, tile, own, other)
    keep = keep_row(pos_ref, levels_ref, tile.shape[1])
    rect = jnp.maximum(dot(w_ref[...], tile[...], TN), 0.0)
    rect_ref[...] = rect
    sq_ref[...] = (rect * rect * keep).astype(BF16)
    hand_out(pos_ref, tile, blk_ref, (s1, s2, s3), 0, share)


def down_kernel(share, pos_ref, levels_ref, own, other, w_ref, rect_ref, t1, t2, t3, hid_ref, blk_ref, s1, s2, s3, tile):
    lay_out(pos_ref, tile, own, other)
    keep = keep_row(pos_ref, levels_ref, tile.shape[1])
    grad = dot(w_ref[...], tile[...], NN)
    hid_ref[...] = (grad * 2.0 * rect_ref[...] * keep).astype(BF16)
    hand_out(pos_ref, tile, blk_ref, (s1, s2, s3), share, share)
    for t, s in ((t1, s1), (t2, s2), (t3, s3)):
        s[:share, :] = t[...]


def back_kernel(pos_ref, w_ref, w_other_ref, hid_ref, hid_other_ref, *outs):
    z, core = pos_ref[0], pos_ref[1]
    height = outs[0].shape[0]
    for k in range(8):
        chip = lax.rem(z + k, 8)
        rows = pl.ds(pl.multiple_of(chip * (2 * height) + core * height, 64), height)
        term = dot(w_ref[rows, :], hid_ref[...], NN) + dot(w_other_ref[rows, :], hid_other_ref[...], NN)
        outs[k][...] = term.astype(BF16)
    half = height // 2
    outs[8][...] = outs[4][:half, :]
    outs[9][...] = outs[4][half:, :]


def wgrad_kernel(scale, flip, base, share, pos_ref, blk_own, col, col_other, h_own, h_l, h_r, h_o1, h_o2, out_ref, blk):
    core = pos_ref[1]
    per_group = col.shape[1] // 3
    h_o = jnp.concatenate([h_o1[...], h_o2[...]], axis=0)

    def term(h, block):
        return dot(h, block, NT) if flip else dot(block, h, NT)

    acc = term(h_own[...], blk_own[...])
    for g, h in enumerate((h_l[...], h_r[...], h_o)):
        source = slice(g * per_group + base, g * per_group + base + share)
        for chip in range(8):
            first = chip * 2 * share
            blk[g, pl.ds(pl.multiple_of(first + core * share, 16), share), :] = col[chip, source, :]
            blk[g, pl.ds(pl.multiple_of(first + (1 - core) * share, 16), share), :] = col_other[chip, source, :]
        acc += term(h, blk[g])
    out_ref[...] = (acc * scale).astype(BF16)


def spread(sends):
    return jnp.concatenate(
        [shift(sends[0], "dp", 1), shift(sends[2], "dp", -1), shift(sends[1], "dp", 2)]
    )


def plus(a, b):
    return (a.astype(F32) + b.astype(F32)).astype(BF16)


def shards(tokens, cotangent, w_in, w_out, levels):
    z, core, dp = lax.axis_index("z"), lax.axis_index("core"), lax.axis_index("dp")
    pos = jnp.stack([z, core, dp]).astype(jnp.int32)
    w_in, w_out, levels = w_in[0], w_out[0], levels[0]
    d, f = w_in.shape
    t, width = tokens.shape[1:]
    rows = d // 4
    share = rows // 16
    flops = 2 * t * d * f

    w_other = shift(w_in, "core", 1)
    tok = column(pos, ring_gather(tokens[0].T), "tok_column")
    tok_other = shift(tok, "core", 1)
    cot = column(pos, ring_gather(cotangent[0].T), "cot_column")
    cot_other = shift(cot, "core", 1)
    w_in, w_other = lax.optimization_barrier((w_in, w_other))

    tile = [pltpu.VMEM((d, t), BF16)]
    rect, sq, tok_blk, *tok_sends = pl.pallas_call(
        functools.partial(up_kernel, share),
        out_shape=(sds(f, t, dtype=F32), sds(f, t), sds(rows, t)) + (sds(share, t),) * 3,
        in_specs=[SMEM, SMEM] + [VMEM] * 3,
        out_specs=[VMEM] * 6,
        scratch_shapes=tile,
        compiler_params=params(),
        cost_estimate=cost(flops, 12 * MIB),
        name="up",
    )(pos, levels, tok, tok_other, w_in)
    sq_l, sq_r = both(sq, sq, "dp")
    hid, cot_blk, *sends = pl.pallas_call(
        functools.partial(down_kernel, share),
        out_shape=(sds(f, t), sds(rows, t)) + (sds(2 * share, t),) * 3,
        in_specs=[SMEM, SMEM] + [VMEM] * 7,
        out_specs=[VMEM] * 5,
        scratch_shapes=tile,
        compiler_params=params(),
        cost_estimate=cost(flops, 12 * MIB),
        name="down",
    )(pos, levels, cot, cot_other, w_out, rect, *tok_sends)
    hid_other = shift(hid, "core", 1)
    hid_l, hid_r = both(hid, hid, "dp")

    piece = spread(sends)
    cut = piece.shape[0] // 2
    l1, r1 = both(piece, piece, "z")
    l2, r2 = both(l1, r1, "z")
    l2, sq_l, sq_r = lax.optimization_barrier((l2, sq_l, sq_r))
    l3, r3 = both(l2, r2, "z")
    half = f // 2
    sq_o1, sq_o2 = both(sq_l[:half], sq_r[half:], "dp")
    hid_other = after(hid_other, l2, r2)
    terms = pl.pallas_call(
        back_kernel,
        out_shape=(sds(width, t),) * 8 + (sds(width // 2, t),) * 2,
        in_specs=[SMEM] + [VMEM] * 4,
        out_specs=[VMEM] * 10,
        compiler_params=params(),
        cost_estimate=cost(flops, 10 * MIB),
        name="back",
    )(pos, w_in, w_other, hid, hid_other)
    right, left = both(terms[8], terms[9], "z")
    l3 = after(l3, *terms)
    l4, r4 = both(l3[:cut], r3[cut:], "z")
    right = after(right, l3, r3)
    right, left = both(
        plus(terms[3], jnp.pad(right, ((0, width // 2), (0, 0)))),
        plus(terms[5], jnp.pad(left, ((width // 2, 0), (0, 0)))),
        "z",
    )
    blocks = column(pos, (piece, l1, r1, l2, r2, l3, r3, l4, r4), "block_column")
    blocks_other = shift(blocks, "core", 1)
    right = after(right, l4, r4)
    right, left = both(plus(terms[2], right), plus(terms[6], left), "z")
    right, hid_l, hid_r, sq_o1, sq_o2 = lax.optimization_barrier((right, hid_l, hid_r, sq_o1, sq_o2))
    hid_o1, hid_o2 = both(hid_l[:half], hid_r[half:], "dp")
    right, left = both(plus(terms[1], right), plus(terms[7], left), "z")
    input_sum = (terms[0].astype(F32) + right.astype(F32) + left.astype(F32)).astype(BF16)
    sq_all, hid_all = (sq_l, sq_r, sq_o1, sq_o2), (hid_l, hid_r, hid_o1, hid_o2)
    n_pipe = lax.axis_size("pipe")
    received = lax.ppermute(input_sum, "pipe", [(i, i - 1) for i in range(1, n_pipe)])

    scale = 1.0 / math.sqrt(t * lax.axis_size("dp"))

    def wgrad(flip, base, own, h_own, h_all, name):
        return pl.pallas_call(
            functools.partial(wgrad_kernel, scale, flip, base, share),
            out_shape=sds(f, rows) if flip else sds(rows, f),
            in_specs=[SMEM] + [VMEM] * 8,
            out_specs=VMEM,
            scratch_shapes=[pltpu.VMEM((3, rows, t), BF16)],
            compiler_params=params(),
            cost_estimate=cost(flops, 8 * MIB),
            name=name,
        )(pos, own, blocks, blocks_other, h_own, *h_all)

    grad_out = wgrad(True, share, cot_blk, sq, sq_all, "grad_out")
    grad_in = wgrad(False, 0, tok_blk, hid, hid_all, "grad_in")
    return (received.T[None], grad_in[None], grad_out[None])


def solution(mesh):
    n_pipe, n_dp, n_tensor = mesh.devices.shape
    fine = Mesh(mesh.devices.reshape(n_pipe, n_dp, n_tensor // 2, 2), ("pipe", "dp", "z", "core"))
    tensor = ("z", "core")
    return jax.shard_map(
        shards,
        mesh=fine,
        in_specs=(
            P("pipe", "dp", tensor),
            P("pipe", "dp", tensor),
            P("pipe", None, tensor),
            P("pipe", tensor, None),
            P("pipe", "dp"),
        ),
        out_specs=(P("pipe", "dp", tensor), P("pipe", "dp", tensor), P("pipe", tensor, "dp")),
        check_vma=False,
    )
```

```python
import functools
import math

import jax
import jax.numpy as jnp
from jax import lax
from jax.experimental import pallas as pl
from jax.experimental.pallas import tpu as pltpu
from jax.sharding import Mesh
from jax.sharding import PartitionSpec as P

BLOCK = 128
MIB = 1 << 20
F32 = jnp.float32
BF16 = jnp.bfloat16
VMEM = pl.BlockSpec(memory_space=pltpu.VMEM)
SMEM = pl.BlockSpec(memory_space=pltpu.SMEM)
NN = (((1,), (0,)), ((), ()))
NT = (((1,), (1,)), ((), ()))
TN = (((0,), (0,)), ((), ()))


def shift(block, axis, distance):
    n = lax.axis_size(axis)
    return lax.ppermute(block, axis, [(i, (i + distance) % n) for i in range(n)])


def dot(left, right, dims):
    return lax.dot_general(left, right, dims, preferred_element_type=F32)


def both(left, right, axis):
    return shift(left, axis, 1), shift(right, axis, -1)


def params(mib=14):
    return pltpu.CompilerParams(vmem_limit_bytes=mib * MIB)


def cost(flops, nbytes):
    return pl.CostEstimate(flops=flops, bytes_accessed=nbytes, transcendentals=0)


def sds(*shape, dtype=BF16):
    return jax.ShapeDtypeStruct(shape, dtype)


OFFSETS = (0, -1, 1, -2, 2, -3, 3)


def put_column(pos_ref, out_ref, pieces):
    for k, piece in zip(OFFSETS, pieces):
        out_ref[lax.rem(pos_ref[0] + (k + 8), 8)] = piece[...]


def inputs_kernel(share, pos_ref, *refs):
    tok_pieces, cot_pieces, (far_l, far_r) = refs[:7], refs[7:14], refs[14:16]
    tok_ref, cot_ref, *sends = refs[16:]
    z, dp = pos_ref[0], pos_ref[2]
    opposite = lax.rem(z + 4, 8)
    half = far_l.shape[0] // 2
    for n, (out_ref, pieces) in enumerate(((tok_ref, tok_pieces), (cot_ref, cot_pieces))):
        put_column(pos_ref, out_ref, pieces)
        out_ref[opposite, :half] = far_l[n * half : (n + 1) * half, :]
        out_ref[opposite, half:] = far_r[n * half : (n + 1) * half, :]
        first = pl.multiple_of(lax.rem(z, 4) * share, 16)
        for d, send in zip((1, 2, 3), sends):
            chip = lax.rem(dp + d, 4) * 2 + z // 4
            send[n * share : (n + 1) * share, :] = out_ref[chip, pl.ds(first, share), :]


def blocks_kernel(pos_ref, *refs):
    *pieces, far_l, far_r, out_ref = refs
    put_column(pos_ref, out_ref, pieces)
    opposite = lax.rem(pos_ref[0] + 4, 8)
    half = far_l.shape[0]
    out_ref[opposite, :half] = far_l[...]
    out_ref[opposite, half:] = far_r[...]


def lay_out(pos_ref, tile, own, other):
    core = pos_ref[1]
    height = own.shape[1]
    for chip in range(8):
        base = chip * 2 * height
        tile[pl.ds(pl.multiple_of(base + core * height, 64), height), :] = own[chip]
        tile[pl.ds(pl.multiple_of(base + (1 - core) * height, 64), height), :] = other[chip]


def keep_row(pos_ref, levels_ref, tokens):
    rank = pos_ref[0] * 2 + pos_ref[1]
    return jnp.concatenate(
        [
            jnp.full((1, BLOCK), (levels_ref[b] > rank).astype(F32), F32)
            for b in range(tokens // BLOCK)
        ],
        axis=1,
    )


def own_rows(pos_ref, tile, blk_ref):
    rows = blk_ref.shape[0]
    blk_ref[...] = tile[pl.ds(pl.multiple_of(pos_ref[2] * rows, 64), rows), :]


def up_kernel(pos_ref, levels_ref, own, other, w_ref, rect_ref, sq_ref, blk_ref, tile):
    lay_out(pos_ref, tile, own, other)
    keep = keep_row(pos_ref, levels_ref, tile.shape[1])
    rect = jnp.maximum(dot(w_ref[...], tile[...], TN), 0.0)
    rect_ref[...] = rect
    sq_ref[...] = (rect * rect * keep).astype(BF16)
    own_rows(pos_ref, tile, blk_ref)


def down_kernel(pos_ref, levels_ref, own, other, w_ref, rect_ref, hid_ref, blk_ref, tile):
    lay_out(pos_ref, tile, own, other)
    keep = keep_row(pos_ref, levels_ref, tile.shape[1])
    grad = dot(w_ref[...], tile[...], NN)
    hid_ref[...] = (grad * 2.0 * rect_ref[...] * keep).astype(BF16)
    own_rows(pos_ref, tile, blk_ref)


def back_kernel(pos_ref, w_ref, w_other_ref, hid_ref, hid_other_ref, *outs):
    z, core = pos_ref[0], pos_ref[1]
    height = outs[0].shape[0]
    for k in range(8):
        chip = lax.rem(z + k, 8)
        rows = pl.ds(pl.multiple_of(chip * (2 * height) + core * height, 64), height)
        term = dot(w_ref[rows, :], hid_ref[...], NN) + dot(w_other_ref[rows, :], hid_other_ref[...], NN)
        outs[k][...] = term.astype(BF16)
    half = height // 2
    outs[8][...] = outs[4][:half, :]
    outs[9][...] = outs[4][half:, :]


def wgrad_kernel(scale, flip, base, share, pos_ref, blk_own, col, col_other, *refs):
    *hidden, far_l, far_r, out_ref, blk = refs
    core = pos_ref[1]
    per_group = col.shape[1] // 3
    for g in range(3):
        source = slice(g * per_group + base, g * per_group + base + share)
        for chip in range(8):
            first = chip // 4 * (8 * share) + chip % 4 * share
            blk[g, pl.ds(pl.multiple_of(first + core * (4 * share), 16), share), :] = col[chip, source, :]
            blk[g, pl.ds(pl.multiple_of(first + (1 - core) * (4 * share), 16), share), :] = col_other[chip, source, :]
    half = far_l.shape[0]
    for n, far in enumerate((far_l, far_r)):
        part = slice(n * half, (n + 1) * half)
        acc = None
        for g, h in enumerate((*(h[part, :] for h in hidden), far[...])):
            block = blk_own[...] if g == 0 else blk[g - 1]
            term = dot(h, block, NT) if flip else dot(block, h, NT)
            acc = term if acc is None else acc + term
        if flip:
            out_ref[part, :] = (acc * scale).astype(BF16)
        else:
            out_ref[:, part] = (acc * scale).astype(BF16)


def plus(a, b):
    return (a.astype(F32) + b.astype(F32)).astype(BF16)


def shards(tokens, cotangent, w_in, w_out, levels):
    z, core, dp = lax.axis_index("z"), lax.axis_index("core"), lax.axis_index("dp")
    pos = jnp.stack([z, core, dp]).astype(jnp.int32)
    w_in, w_out, levels = w_in[0], w_out[0], levels[0]
    d, f = w_in.shape
    t, width = tokens.shape[1:]
    rows = d // 4
    share = rows // 16
    half, cut = f // 2, width // 2
    flops = 2 * t * d * f

    def call(kernel, out_shape, n_scalars, operands, scratch=(), work=0, name=None):
        return pl.pallas_call(
            kernel,
            out_shape=out_shape,
            in_specs=[SMEM] * n_scalars + [VMEM] * (len(operands) - n_scalars),
            out_specs=jax.tree.map(lambda _: VMEM, out_shape),
            scratch_shapes=scratch,
            compiler_params=params(),
            cost_estimate=cost(work, work // 256),
            name=name,
        )(*operands)

    w_other = shift(w_in, "core", 1)
    tok, cot = tokens[0].T, cotangent[0].T
    tok_ring, cot_ring = [(tok, tok)], [(cot, cot)]
    for _ in range(3):
        tok_ring.append(both(*tok_ring[-1], "z"))
        cot_ring.append(both(*cot_ring[-1], "z"))
    (tok_l, tok_r), (cot_l, cot_r) = tok_ring[-1], cot_ring[-1]
    far = both(
        jnp.concatenate([tok_l[:cut], cot_l[:cut]]), jnp.concatenate([tok_r[cut:], cot_r[cut:]]), "z"
    )
    tok_pieces = (tok, *(p for pair in tok_ring[1:] for p in pair))
    cot_pieces = (cot, *(p for pair in cot_ring[1:] for p in pair))
    tok, cot, *sends = call(
        functools.partial(inputs_kernel, share),
        (sds(8, width, t), sds(8, width, t)) + (sds(2 * share, t),) * 3,
        1,
        (pos, *tok_pieces, *cot_pieces, *far),
        name="inputs",
    )
    tok_other = shift(tok, "core", 1)
    cot_other = shift(cot, "core", 1)
    piece = jnp.concatenate(
        [shift(sends[0], "dp", 1), shift(sends[2], "dp", -1), shift(sends[1], "dp", 2)]
    )
    w_in, w_other = lax.optimization_barrier((w_in, w_other))

    tile = [pltpu.VMEM((d, t), BF16)]
    rect, sq, tok_blk = call(
        up_kernel,
        (sds(f, t, dtype=F32), sds(f, t), sds(rows, t)),
        2,
        (pos, levels, tok, tok_other, w_in),
        tile,
        name="up",
    )
    hid, cot_blk = call(
        down_kernel,
        (sds(f, t), sds(rows, t)),
        2,
        (pos, levels, cot, cot_other, w_out, rect),
        tile,
        name="down",
    )

    sq_l, sq_r = both(sq, sq, "dp")
    hid_other = shift(hid, "core", 1)
    hid_l, hid_r = both(hid, hid, "dp")
    ring = [(piece, piece)]
    for _ in range(3):
        ring.append(both(*ring[-1], "z"))
    far_l, sq_l, sq_r = lax.optimization_barrier((ring[-1][0], sq_l, sq_r))
    part = piece.shape[0] // 2
    far = both(far_l[:part], ring[-1][1][part:], "z")
    sq_ol, sq_or = both(sq_l[:half], sq_r[half:], "dp")
    terms = call(
        back_kernel,
        (sds(width, t),) * 8 + (sds(cut, t),) * 2,
        1,
        (pos, w_in, w_other, hid, hid_other),
        name="back",
    )
    right, left = both(terms[8], terms[9], "z")
    right, hid_l, hid_r = lax.optimization_barrier((right, hid_l, hid_r))
    hid_ol, hid_or = both(hid_l[:half], hid_r[half:], "dp")
    right, left = both(
        plus(terms[3], jnp.pad(right, ((0, cut), (0, 0)))),
        plus(terms[5], jnp.pad(left, ((cut, 0), (0, 0)))),
        "z",
    )
    right, left = both(plus(terms[2], right), plus(terms[6], left), "z")
    right, sq_ol, sq_or = lax.optimization_barrier((right, sq_ol, sq_or))
    right, left = both(plus(terms[1], right), plus(terms[7], left), "z")
    input_sum = (terms[0].astype(F32) + right.astype(F32) + left.astype(F32)).astype(BF16)

    blocks = call(
        blocks_kernel,
        sds(8, *piece.shape),
        1,
        (pos, piece, *(p for pair in ring[1:] for p in pair), *far),
        name="blocks",
    )
    blocks_other = shift(blocks, "core", 1)
    scale = 1.0 / math.sqrt(t * lax.axis_size("dp"))

    def wgrad(flip, base, own, hidden, name):
        return call(
            functools.partial(wgrad_kernel, scale, flip, base, share),
            sds(f, rows) if flip else sds(rows, f),
            1,
            (pos, own, blocks, blocks_other, *hidden),
            [pltpu.VMEM((3, rows, t), BF16)],
            2 * flops,
            name=name,
        )

    grad_out = wgrad(True, share, cot_blk, (sq, sq_l, sq_r, sq_ol, sq_or), "grad_out")
    input_sum, hid_ol, hid_or, grad_out = lax.optimization_barrier((input_sum, hid_ol, hid_or, grad_out))
    grad_in = wgrad(False, 0, tok_blk, (hid, hid_l, hid_r, hid_ol, hid_or), "grad_in")
    n_pipe = lax.axis_size("pipe")
    received = lax.ppermute(input_sum, "pipe", [(i, i - 1) for i in range(1, n_pipe)])
    return (received.T[None], grad_in[None], grad_out[None])


def solution(mesh):
    n_pipe, n_dp, n_tensor = mesh.devices.shape
    fine = Mesh(mesh.devices.reshape(n_pipe, n_dp, n_tensor // 2, 2), ("pipe", "dp", "z", "core"))
    tensor = ("z", "core")
    return jax.shard_map(
        shards,
        mesh=fine,
        in_specs=(
            P("pipe", "dp", tensor),
            P("pipe", "dp", tensor),
            P("pipe", None, tensor),
            P("pipe", tensor, None),
            P("pipe", "dp"),
        ),
        out_specs=(P("pipe", "dp", tensor), P("pipe", "dp", tensor), P("pipe", tensor, "dp")),
        check_vma=False,
    )
```

```python
import functools
import math

import jax
import jax.numpy as jnp
from jax import lax
from jax.experimental import pallas as pl
from jax.experimental.pallas import tpu as pltpu
from jax.sharding import Mesh
from jax.sharding import PartitionSpec as P

BLOCK = 128
TILE = 256
MIB = 1 << 20
F32 = jnp.float32
BF16 = jnp.bfloat16
VMEM = pl.BlockSpec(memory_space=pltpu.VMEM)
HBM = pl.BlockSpec(memory_space=pltpu.HBM)
SMEM = pl.BlockSpec(memory_space=pltpu.SMEM)
NN = (((1,), (0,)), ((), ()))
NT = (((1,), (1,)), ((), ()))
TN = (((0,), (0,)), ((), ()))


def shift(block, axis, distance):
    n = lax.axis_size(axis)
    return lax.ppermute(block, axis, [(i, (i + distance) % n) for i in range(n)])


def dot(left, right, dims):
    return lax.dot_general(left, right, dims, preferred_element_type=F32)


def both(left, right, axis):
    return shift(left, axis, 1), shift(right, axis, -1)


def params(mib=18):
    return pltpu.CompilerParams(vmem_limit_bytes=mib * MIB)


def cost(flops, nbytes):
    return pl.CostEstimate(flops=flops, bytes_accessed=nbytes, transcendentals=0)


def sds(*shape, dtype=BF16):
    return jax.ShapeDtypeStruct(shape, dtype)


OFFSETS = (0, -1, 1, -2, 2, -3, 3)


def put_column(pos_ref, out_ref, pieces):
    for k, piece in zip(OFFSETS, pieces):
        out_ref[lax.rem(pos_ref[0] + (k + 8), 8)] = piece[...]


def inputs_kernel(share, pos_ref, *refs):
    tok_pieces, cot_pieces, (far_l, far_r) = refs[:7], refs[7:14], refs[14:16]
    tok_ref, cot_ref, *sends = refs[16:]
    z, dp = pos_ref[0], pos_ref[2]
    opposite = lax.rem(z + 4, 8)
    half = far_l.shape[0] // 2
    for n, (out_ref, pieces) in enumerate(((tok_ref, tok_pieces), (cot_ref, cot_pieces))):
        put_column(pos_ref, out_ref, pieces)
        out_ref[opposite, :half] = far_l[n * half : (n + 1) * half, :]
        out_ref[opposite, half:] = far_r[n * half : (n + 1) * half, :]
        first = pl.multiple_of(lax.rem(z, 4) * share, 16)
        for d, send in zip((1, 2, 3), sends):
            chip = lax.rem(dp + d, 4) * 2 + z // 4
            send[n * share : (n + 1) * share, :] = out_ref[chip, pl.ds(first, share), :]


def blocks_kernel(pos_ref, *refs):
    *pieces, far_l, far_r, out_ref = refs
    put_column(pos_ref, out_ref, pieces)
    opposite = lax.rem(pos_ref[0] + 4, 8)
    half = far_l.shape[0]
    out_ref[opposite, :half] = far_l[...]
    out_ref[opposite, half:] = far_r[...]


def lay_out(pos_ref, tile, own, other):
    core = pos_ref[1]
    height = own.shape[1]
    for chip in range(8):
        base = chip * 2 * height
        tile[pl.ds(pl.multiple_of(base + core * height, 64), height), :] = own[chip]
        tile[pl.ds(pl.multiple_of(base + (1 - core) * height, 64), height), :] = other[chip]


def keep_row(pos_ref, levels_ref, tokens):
    rank = pos_ref[0] * 2 + pos_ref[1]
    return jnp.concatenate(
        [
            jnp.full((1, BLOCK), (levels_ref[b] > rank).astype(F32), F32)
            for b in range(tokens // BLOCK)
        ],
        axis=1,
    )


def own_rows(pos_ref, tile, blk_ref):
    rows = blk_ref.shape[0]
    blk_ref[...] = tile[pl.ds(pl.multiple_of(pos_ref[2] * rows, 64), rows), :]


def fetch(w_hbm, w_ref, sem):
    copies = [pltpu.make_async_copy(src, dst, sem.at[n]) for n, (src, dst) in enumerate(zip(w_hbm, w_ref))]
    for copy in copies:
        copy.start()
    return copies


def up_kernel(pos_ref, levels_ref, own, other, w_hbm, rect_ref, sq_ref, blk_ref, tile, w_ref, sem):
    copies = fetch(
        [w_hbm.at[:, n * TILE : (n + 1) * TILE] for n in range(w_ref.shape[0])],
        [w_ref.at[n] for n in range(w_ref.shape[0])],
        sem,
    )
    lay_out(pos_ref, tile, own, other)
    own_rows(pos_ref, tile, blk_ref)
    keep = keep_row(pos_ref, levels_ref, tile.shape[1])
    for copy in copies:
        copy.wait()

    @pl.loop(0, w_ref.shape[0])
    def _(n):
        part = pl.ds(pl.multiple_of(n * TILE, TILE), TILE)
        rect = jnp.maximum(dot(w_ref[n], tile[...], TN), 0.0)
        rect_ref[part, :] = rect
        sq_ref[part, :] = (rect * rect * keep).astype(BF16)


def down_kernel(pos_ref, levels_ref, own, other, w_hbm, rect_ref, hid_ref, blk_ref, tile, w_ref, sem):
    copies = fetch(
        [w_hbm.at[n * TILE : (n + 1) * TILE, :] for n in range(w_ref.shape[0])],
        [w_ref.at[n] for n in range(w_ref.shape[0])],
        sem,
    )
    lay_out(pos_ref, tile, own, other)
    own_rows(pos_ref, tile, blk_ref)
    keep = keep_row(pos_ref, levels_ref, tile.shape[1])
    for copy in copies:
        copy.wait()

    @pl.loop(0, w_ref.shape[0])
    def _(n):
        part = pl.ds(pl.multiple_of(n * TILE, TILE), TILE)
        grad = dot(w_ref[n], tile[...], NN)
        hid_ref[part, :] = (grad * 2.0 * rect_ref[part, :] * keep).astype(BF16)


def back_kernel(pos_ref, w_ref, w_other_ref, hid_ref, hid_other_ref, out_ref):
    z, core = pos_ref[0], pos_ref[1]
    height = out_ref.shape[1]

    @pl.loop(0, 8)
    def _(k):
        first = lax.rem(z + k, 8) * (2 * height) + core * height
        rows = pl.ds(pl.multiple_of(first, 64), height)
        term = dot(w_ref[rows, :], hid_ref[...], NN) + dot(w_other_ref[rows, :], hid_other_ref[...], NN)
        out_ref[k] = term.astype(BF16)


def wgrad_kernel(scale, flip, base, share, pos_ref, blk_own, col, col_other, *refs):
    *hidden, far_l, far_r, out_ref, blk, far = refs
    core = pos_ref[1]
    per_group = col.shape[1] // 3
    for g in range(3):
        source = slice(g * per_group + base, g * per_group + base + share)
        for chip in range(8):
            first = chip // 4 * (8 * share) + chip % 4 * share
            blk[g, pl.ds(pl.multiple_of(first + core * (4 * share), 16), share), :] = col[chip, source, :]
            blk[g, pl.ds(pl.multiple_of(first + (1 - core) * (4 * share), 16), share), :] = col_other[chip, source, :]
    half = far_l.shape[0]
    far[:half, :] = far_l[...]
    far[half:, :] = far_r[...]

    @pl.loop(0, far.shape[0] // TILE)
    def _(n):
        part = pl.ds(pl.multiple_of(n * TILE, TILE), TILE)
        acc = None
        for g, h in enumerate((*hidden, far)):
            block = blk_own[...] if g == 0 else blk[g - 1]
            term = dot(h[part, :], block, NT) if flip else dot(block, h[part, :], NT)
            acc = term if acc is None else acc + term
        if flip:
            out_ref[part, :] = (acc * scale).astype(BF16)
        else:
            out_ref[:, part] = (acc * scale).astype(BF16)


def plus(a, b):
    return (a.astype(F32) + b.astype(F32)).astype(BF16)


def shards(tokens, cotangent, w_in, w_out, levels):
    z, core, dp = lax.axis_index("z"), lax.axis_index("core"), lax.axis_index("dp")
    pos = jnp.stack([z, core, dp]).astype(jnp.int32)
    w_in, w_out, levels = w_in[0], w_out[0], levels[0]
    d, f = w_in.shape
    t, width = tokens.shape[1:]
    rows = d // 4
    share = rows // 16
    half, cut = f // 2, width // 2
    flops = 2 * t * d * f

    def call(kernel, out_shape, n_scalars, operands, scratch=(), work=0, weight=None, name=None):
        return pl.pallas_call(
            kernel,
            out_shape=out_shape,
            in_specs=[
                SMEM if n < n_scalars else HBM if n == weight else VMEM for n in range(len(operands))
            ],
            out_specs=jax.tree.map(lambda _: VMEM, out_shape),
            scratch_shapes=scratch,
            compiler_params=params(),
            cost_estimate=cost(work, work // 256),
            name=name,
        )(*operands)

    w_other = shift(w_in, "core", 1)
    tok, cot = tokens[0].T, cotangent[0].T
    tok_ring, cot_ring = [(tok, tok)], [(cot, cot)]
    for _ in range(3):
        tok_ring.append(both(*tok_ring[-1], "z"))
        cot_ring.append(both(*cot_ring[-1], "z"))
    (tok_l, tok_r), (cot_l, cot_r) = tok_ring[-1], cot_ring[-1]
    far = both(
        jnp.concatenate([tok_l[:cut], cot_l[:cut]]), jnp.concatenate([tok_r[cut:], cot_r[cut:]]), "z"
    )
    tok_pieces = (tok, *(p for pair in tok_ring[1:] for p in pair))
    cot_pieces = (cot, *(p for pair in cot_ring[1:] for p in pair))
    tok, cot, *sends = call(
        functools.partial(inputs_kernel, share),
        (sds(8, width, t), sds(8, width, t)) + (sds(2 * share, t),) * 3,
        1,
        (pos, *tok_pieces, *cot_pieces, *far),
        name="inputs",
    )
    tok_other = shift(tok, "core", 1)
    shares = shift(sends[0], "dp", 1), shift(sends[2], "dp", -1), shift(sends[1], "dp", 2)
    w_in, w_other = lax.optimization_barrier((w_in, w_other))

    n_tiles = f // TILE
    tile = pltpu.VMEM((d, t), BF16)
    tile_sems = pltpu.SemaphoreType.DMA((n_tiles,))
    rect, sq, tok_blk = call(
        up_kernel,
        (sds(f, t, dtype=F32), sds(f, t), sds(rows, t)),
        2,
        (pos, levels, tok, tok_other, pltpu.with_memory_space_constraint(w_in, pltpu.HBM)),
        [tile, pltpu.VMEM((n_tiles, d, TILE), BF16), tile_sems],
        2 * flops,
        4,
        name="up",
    )
    cot, sq_sent, *shares = lax.optimization_barrier((cot, sq, *shares))
    cot_other = shift(cot, "core", 1)
    hid, cot_blk = call(
        down_kernel,
        (sds(f, t), sds(rows, t)),
        2,
        (pos, levels, cot, cot_other, pltpu.with_memory_space_constraint(w_out, pltpu.HBM), rect),
        [tile, pltpu.VMEM((n_tiles, TILE, d), BF16), tile_sems],
        0,
        4,
        name="down",
    )

    hid_other = shift(hid, "core", 1)
    sq_l, sq_r = both(sq_sent, sq_sent, "dp")
    hid_l, hid_r = both(hid, hid, "dp")
    piece = jnp.concatenate(shares)
    l1, r1 = both(piece, piece, "z")
    l1, r1, _ = lax.optimization_barrier((l1, r1, hid))
    l2, r2 = both(l1, r1, "z")
    terms = call(
        back_kernel, sds(8, width, t), 1, (pos, w_in, w_other, hid, hid_other), (), 2 * flops, name="back"
    )
    l2, r2, sq_l, sq_r, terms = lax.optimization_barrier((l2, r2, sq_l, sq_r, terms))
    right, left = both(terms[4, :cut], terms[4, cut:], "z")
    l3, r3 = both(l2, r2, "z")
    l3, r3, right, left = lax.optimization_barrier((l3, r3, right, left))
    sq_ol, sq_or = both(sq_l[:half], sq_r[half:], "dp")
    part = piece.shape[0] // 2
    far = both(l3[:part], r3[part:], "z")
    right, left = both(
        plus(terms[3], jnp.pad(right, ((0, cut), (0, 0)))),
        plus(terms[5], jnp.pad(left, ((cut, 0), (0, 0)))),
        "z",
    )
    far, right, left, hid_l, hid_r = lax.optimization_barrier((far, right, left, hid_l, hid_r))
    hid_ol, hid_or = both(hid_l[:half], hid_r[half:], "dp")
    right, left = both(plus(terms[2], right), plus(terms[6], left), "z")
    right, left, sq_ol, sq_or = lax.optimization_barrier((right, left, sq_ol, sq_or))
    right, left = both(plus(terms[1], right), plus(terms[7], left), "z")
    input_sum = (terms[0].astype(F32) + right.astype(F32) + left.astype(F32)).astype(BF16)

    blocks = call(
        blocks_kernel,
        sds(8, *piece.shape),
        1,
        (pos, piece, l1, r1, l2, r2, l3, r3, *far),
        name="blocks",
    )
    blocks_other = shift(blocks, "core", 1)
    scale = 1.0 / math.sqrt(t * lax.axis_size("dp"))

    def wgrad(flip, base, own, hidden, name):
        return call(
            functools.partial(wgrad_kernel, scale, flip, base, share),
            sds(f, rows) if flip else sds(rows, f),
            1,
            (pos, own, blocks, blocks_other, *hidden),
            [pltpu.VMEM((3, rows, t), BF16), pltpu.VMEM((f, t), BF16)],
            2 * flops,
            name=name,
        )

    grad_out = wgrad(True, share, cot_blk, (sq, sq_l, sq_r, sq_ol, sq_or), "grad_out")
    input_sum, hid_ol, hid_or, grad_out = lax.optimization_barrier((input_sum, hid_ol, hid_or, grad_out))
    grad_in = wgrad(False, 0, tok_blk, (hid, hid_l, hid_r, hid_ol, hid_or), "grad_in")
    n_pipe = lax.axis_size("pipe")
    received = lax.ppermute(input_sum, "pipe", [(i, i - 1) for i in range(1, n_pipe)])
    return (received.T[None], grad_in[None], grad_out[None])


def solution(mesh):
    n_pipe, n_dp, n_tensor = mesh.devices.shape
    fine = Mesh(mesh.devices.reshape(n_pipe, n_dp, n_tensor // 2, 2), ("pipe", "dp", "z", "core"))
    tensor = ("z", "core")
    return jax.shard_map(
        shards,
        mesh=fine,
        in_specs=(
            P("pipe", "dp", tensor),
            P("pipe", "dp", tensor),
            P("pipe", None, tensor),
            P("pipe", tensor, None),
            P("pipe", "dp"),
        ),
        out_specs=(P("pipe", "dp", tensor), P("pipe", "dp", tensor), P("pipe", tensor, "dp")),
        check_vma=False,
    )
```

```python
import functools
import math

import jax
import jax.numpy as jnp
from jax import lax
from jax.experimental import pallas as pl
from jax.experimental.pallas import tpu as pltpu
from jax.sharding import Mesh
from jax.sharding import PartitionSpec as P

BLOCK = 128
MIB = 1 << 20
F32 = jnp.float32
BF16 = jnp.bfloat16
VMEM = pl.BlockSpec(memory_space=pltpu.VMEM)
HBM = pl.BlockSpec(memory_space=pltpu.HBM)
SMEM = pl.BlockSpec(memory_space=pltpu.SMEM)
NN = (((1,), (0,)), ((), ()))
NT = (((1,), (1,)), ((), ()))
TN = (((0,), (0,)), ((), ()))


def shift(block, axis, distance):
    n = lax.axis_size(axis)
    return lax.ppermute(block, axis, [(i, (i + distance) % n) for i in range(n)])


def dot(left, right, dims):
    return lax.dot_general(left, right, dims, preferred_element_type=F32)


def both(left, right, axis):
    return shift(left, axis, 1), shift(right, axis, -1)


def params(mib=26):
    return pltpu.CompilerParams(vmem_limit_bytes=mib * MIB)


def cost(flops, nbytes):
    return pl.CostEstimate(flops=flops, bytes_accessed=nbytes, transcendentals=0)


def sds(*shape, dtype=BF16):
    return jax.ShapeDtypeStruct(shape, dtype)


OFFSETS = (0, -1, 1, -2, 2, -3, 3)


def put_column(pos_ref, out_ref, pieces):
    for k, piece in zip(OFFSETS, pieces):
        out_ref[lax.rem(pos_ref[0] + (k + 8), 8)] = piece[...]


def inputs_kernel(share, pos_ref, *refs):
    tok_pieces, cot_pieces, (far_l, far_r) = refs[:7], refs[7:14], refs[14:16]
    tok_ref, cot_ref, *sends = refs[16:]
    z, dp = pos_ref[0], pos_ref[2]
    opposite = lax.rem(z + 4, 8)
    half = far_l.shape[0] // 2
    for n, (out_ref, pieces) in enumerate(((tok_ref, tok_pieces), (cot_ref, cot_pieces))):
        put_column(pos_ref, out_ref, pieces)
        out_ref[opposite, :half] = far_l[n * half : (n + 1) * half, :]
        out_ref[opposite, half:] = far_r[n * half : (n + 1) * half, :]
        first = pl.multiple_of(lax.rem(z, 4) * share, 16)
        for d, send in zip((1, 2, 3), sends):
            chip = lax.rem(dp + d, 4) * 2 + z // 4
            send[n * share : (n + 1) * share, :] = out_ref[chip, pl.ds(first, share), :]


def blocks_kernel(pos_ref, *refs):
    *pieces, far_l, far_r, out_ref = refs
    put_column(pos_ref, out_ref, pieces)
    opposite = lax.rem(pos_ref[0] + 4, 8)
    half = far_l.shape[0]
    out_ref[opposite, :half] = far_l[...]
    out_ref[opposite, half:] = far_r[...]


def lay_out(pos_ref, tile, own, other):
    core = pos_ref[1]
    height = own.shape[1]
    for chip in range(8):
        base = chip * 2 * height
        tile[pl.ds(pl.multiple_of(base + core * height, 64), height), :] = own[chip]
        tile[pl.ds(pl.multiple_of(base + (1 - core) * height, 64), height), :] = other[chip]


def keep_row(pos_ref, levels_ref, tokens):
    rank = pos_ref[0] * 2 + pos_ref[1]
    return jnp.concatenate(
        [
            jnp.full((1, BLOCK), (levels_ref[b] > rank).astype(F32), F32)
            for b in range(tokens // BLOCK)
        ],
        axis=1,
    )


def own_rows(pos_ref, tile, blk_ref):
    rows = blk_ref.shape[0]
    blk_ref[...] = tile[pl.ds(pl.multiple_of(pos_ref[2] * rows, 64), rows), :]


def fetch(pairs, sem):
    copies = [pltpu.make_async_copy(src, dst, sem.at[n]) for n, (src, dst) in enumerate(pairs)]
    for copy in copies:
        copy.start()
    return copies


def hidden_kernel(
    pos_ref, levels_ref, tok, tok_other, cot, cot_other, w_in, w_out, hid_ref, bundle_ref, tok_ref, cot_ref, tile, cot_tile, rect_ref, win, wout, sem
):
    n_tiles, size = wout.shape[:2]
    tiles = [slice(n * size, (n + 1) * size) for n in range(n_tiles)]
    copies = fetch(
        [(w_in.at[:, part], win.at[n]) for n, part in enumerate(tiles)]
        + [(w_out.at[part, :], wout.at[n]) for n, part in enumerate(tiles)],
        sem,
    )
    keep = keep_row(pos_ref, levels_ref, tile.shape[1])
    half = hid_ref.shape[0] // 2

    def put(n, block, kind):
        for m in range(2):
            low, high = max(n * size, m * half), min((n + 1) * size, (m + 1) * half)
            if low < high:
                start = (2 * m + kind) * half + low - m * half
                bundle_ref[start : start + high - low, :] = block[low - n * size : high - n * size]

    lay_out(pos_ref, tile, tok, tok_other)
    own_rows(pos_ref, tile, tok_ref)
    for n, part in enumerate(tiles):
        copies[n].wait()
        rect = jnp.maximum(dot(win[n], tile[...], TN), 0.0)
        rect_ref[part, :] = rect
        put(n, (rect * rect * keep).astype(BF16), 0)
    lay_out(pos_ref, cot_tile, cot, cot_other)
    own_rows(pos_ref, cot_tile, cot_ref)
    for n, part in enumerate(tiles):
        copies[n_tiles + n].wait()
        grad = dot(wout[n], cot_tile[...], NN)
        hid = (grad * 2.0 * rect_ref[part, :] * keep).astype(BF16)
        hid_ref[part, :] = hid
        put(n, hid, 1)


def back_kernel(pos_ref, w_ref, w_other_ref, hid_ref, hid_other_ref, out_ref, w, sem):
    z, core = pos_ref[0], pos_ref[1]
    height = out_ref.shape[1]
    rows = []
    for k in range(8):
        first = lax.rem(z + k, 8) * (2 * height) + core * height
        rows.append(pl.ds(pl.multiple_of(first, 64), height))
    copies = fetch([(w_ref.at[rows[k], :], w.at[k]) for k in range(8)], sem)
    for k in range(8):
        copies[k].wait()
        term = dot(w[k], hid_ref[...], NN) + dot(w_other_ref[rows[k], :], hid_other_ref[...], NN)
        out_ref[k] = term.astype(BF16)


def wgrad_kernel(share, pos_ref, tok_blk, cot_blk, col, col_other, *refs):
    *bundles, out_ref, in_ref, tok_far, cot_far, blk = refs
    core = pos_ref[1]
    per_group = col.shape[1] // 3
    for g in range(3):
        for m in range(2):
            source = slice(g * per_group + m * share, g * per_group + (m + 1) * share)
            ref = blk.at[g, m] if g < 2 else (tok_far, cot_far)[m]
            for chip in range(8):
                first = chip // 4 * (8 * share) + chip % 4 * share
                ref[pl.ds(pl.multiple_of(first + core * (4 * share), 16), share), :] = col[chip, source, :]
                ref[pl.ds(pl.multiple_of(first + (1 - core) * (4 * share), 16), share), :] = col_other[chip, source, :]
    half = out_ref.shape[0] // 2
    for n in range(2):
        part = slice(n * half, (n + 1) * half)
        acc_out = acc_in = 0.0
        for g, bundle in enumerate(bundles):
            tok, cot = (tok_blk[...], cot_blk[...]) if g == 0 else (blk[g - 1, 0], blk[g - 1, 1])
            acc_out += dot(bundle[2 * n * half : (2 * n + 1) * half, :], cot, NT)
            acc_in += dot(tok, bundle[(2 * n + 1) * half : (2 * n + 2) * half, :], NT)
        out_ref[part, :] = acc_out
        in_ref[:, part] = acc_in


def last_kernel(scale, acc_out, acc_in, tok_far, cot_far, far_a, far_b, out_ref, in_ref):
    half = far_a.shape[0] // 2
    for n, bundle in enumerate((far_a, far_b)):
        part = slice(n * half, (n + 1) * half)
        out_ref[part, :] = ((acc_out[part, :] + dot(bundle[:half, :], cot_far[...], NT)) * scale).astype(BF16)
        in_ref[:, part] = ((acc_in[:, part] + dot(tok_far[...], bundle[half:, :], NT)) * scale).astype(BF16)


def plus(a, b):
    return (a.astype(F32) + b.astype(F32)).astype(BF16)


def shards(tokens, cotangent, w_in, w_out, levels):
    z, core, dp = lax.axis_index("z"), lax.axis_index("core"), lax.axis_index("dp")
    pos = jnp.stack([z, core, dp]).astype(jnp.int32)
    w_in, w_out, levels = w_in[0], w_out[0], levels[0]
    d, f = w_in.shape
    t, width = tokens.shape[1:]
    rows = d // 4
    share = rows // 16
    half, cut = f // 2, width // 2
    flops = 2 * t * d * f

    def call(kernel, out_shape, n_scalars, operands, scratch=(), work=0, hbm=(), name=None):
        return pl.pallas_call(
            kernel,
            out_shape=out_shape,
            in_specs=[
                SMEM if n < n_scalars else HBM if n in hbm else VMEM for n in range(len(operands))
            ],
            out_specs=jax.tree.map(lambda _: VMEM, out_shape),
            scratch_shapes=scratch,
            compiler_params=params(),
            cost_estimate=cost(work, work // 256),
            name=name,
        )(*(pltpu.with_memory_space_constraint(x, pltpu.HBM) if n in hbm else x for n, x in enumerate(operands)))

    w_other = shift(w_in, "core", 1)
    tok_ring, cot_ring = [(tokens[0].T,) * 2], [(cotangent[0].T,) * 2]
    for _ in range(3):
        tok_ring.append(both(*tok_ring[-1], "z"))
        cot_ring.append(both(*cot_ring[-1], "z"))
    (tok_l, tok_r), (cot_l, cot_r) = tok_ring[-1], cot_ring[-1]
    far = both(
        jnp.concatenate([tok_l[:cut], cot_l[:cut]]), jnp.concatenate([tok_r[cut:], cot_r[cut:]]), "z"
    )
    far, w_other = lax.optimization_barrier((far, w_other))
    tok_pieces = (tok_ring[0][0], *(p for pair in tok_ring[1:] for p in pair))
    cot_pieces = (cot_ring[0][0], *(p for pair in cot_ring[1:] for p in pair))
    tok, cot, *sends = call(
        functools.partial(inputs_kernel, share),
        (sds(8, width, t), sds(8, width, t)) + (sds(2 * share, t),) * 3,
        1,
        (pos, *tok_pieces, *cot_pieces, *far),
        name="inputs",
    )
    tok_other, cot_other = shift(tok, "core", 1), shift(cot, "core", 1)
    shares = shift(sends[0], "dp", 1), shift(sends[2], "dp", -1), shift(sends[1], "dp", 2)
    cot_other, shares = lax.optimization_barrier((cot_other, shares))
    size = 256
    hid, bundle, tok_blk, cot_blk = call(
        hidden_kernel,
        (sds(f, t), sds(2 * f, t), sds(rows, t), sds(rows, t)),
        2,
        (pos, levels, tok, tok_other, cot, cot_other, w_in, w_out),
        [
            pltpu.VMEM((d, t), BF16),
            pltpu.VMEM((d, t), BF16),
            pltpu.VMEM((f, t), F32),
            pltpu.VMEM((f // size, d, size), BF16),
            pltpu.VMEM((f // size, size, d), BF16),
            pltpu.SemaphoreType.DMA((2 * f // size,)),
        ],
        hbm=(6, 7),
        name="hidden",
    )

    hid_other = shift(hid, "core", 1)
    bundle_l, bundle_r = both(bundle, bundle, "dp")
    piece = jnp.concatenate(shares)
    l1, r1 = both(piece, piece, "z")
    terms = call(
        back_kernel,
        sds(8, width, t),
        1,
        (pos, w_in, w_other, hid, hid_other),
        [pltpu.VMEM((8, width, f), BF16), pltpu.SemaphoreType.DMA((8,))],
        2 * flops,
        (1,),
        name="back",
    )
    l1, r1, hid_other = lax.optimization_barrier((l1, r1, hid_other))
    l2, r2 = both(l1, r1, "z")
    l2, r2, terms = lax.optimization_barrier((l2, r2, terms))
    l3, r3 = both(l2, r2, "z")
    part = piece.shape[0] // 2
    far = both(l3[:part], r3[part:], "z")
    right, left = both(terms[4, :cut], terms[4, cut:], "z")
    right, left = lax.optimization_barrier((right, left))
    right, left = both(
        plus(terms[3], jnp.pad(right, ((0, cut), (0, 0)))),
        plus(terms[5], jnp.pad(left, ((cut, 0), (0, 0)))),
        "z",
    )
    right, left, far, bundle_l, bundle_r = lax.optimization_barrier((right, left, far, bundle_l, bundle_r))
    far_a, far_b = both(bundle_l[:f], bundle_r[f:], "dp")
    right, left = both(plus(terms[2], right), plus(terms[6], left), "z")
    right, left = lax.optimization_barrier((right, left))
    right, left = both(plus(terms[1], right), plus(terms[7], left), "z")

    blocks = call(
        blocks_kernel,
        sds(8, *piece.shape),
        1,
        (pos, piece, l1, r1, l2, r2, l3, r3, *far),
        name="blocks",
    )
    blocks_other = shift(blocks, "core", 1)
    scale = 1.0 / math.sqrt(t * lax.axis_size("dp"))

    acc_out, acc_in, tok_far, cot_far = call(
        functools.partial(wgrad_kernel, share),
        (sds(f, rows, dtype=F32), sds(rows, f, dtype=F32), sds(rows, t), sds(rows, t)),
        1,
        (pos, tok_blk, cot_blk, blocks, blocks_other, bundle, bundle_l, bundle_r),
        [pltpu.VMEM((2, 2, rows, t), BF16)],
        flops,
        name="wgrad",
    )
    right, left, acc_out = lax.optimization_barrier((right, left, acc_out))
    input_sum = (terms[0].astype(F32) + right.astype(F32) + left.astype(F32)).astype(BF16)
    grad_out, grad_in = call(
        functools.partial(last_kernel, scale),
        (sds(f, rows), sds(rows, f)),
        0,
        (acc_out, acc_in, tok_far, cot_far, far_a, far_b),
        name="last",
    )
    n_pipe = lax.axis_size("pipe")
    received = lax.ppermute(input_sum, "pipe", [(i, i - 1) for i in range(1, n_pipe)])
    return (received.T[None], grad_in[None], grad_out[None])


def solution(mesh):
    n_pipe, n_dp, n_tensor = mesh.devices.shape
    fine = Mesh(mesh.devices.reshape(n_pipe, n_dp, n_tensor // 2, 2), ("pipe", "dp", "z", "core"))
    tensor = ("z", "core")
    return jax.shard_map(
        shards,
        mesh=fine,
        in_specs=(
            P("pipe", "dp", tensor),
            P("pipe", "dp", tensor),
            P("pipe", None, tensor),
            P("pipe", tensor, None),
            P("pipe", "dp"),
        ),
        out_specs=(P("pipe", "dp", tensor), P("pipe", "dp", tensor), P("pipe", tensor, "dp")),
        check_vma=False,
    )
```

```python
import functools
import math

import jax
import jax.numpy as jnp
from jax import lax
from jax.experimental import pallas as pl
from jax.experimental.pallas import tpu as pltpu
from jax.sharding import Mesh
from jax.sharding import PartitionSpec as P

BLOCK = 128
MIB = 1 << 20
F32 = jnp.float32
BF16 = jnp.bfloat16
VMEM = pl.BlockSpec(memory_space=pltpu.VMEM)
HBM = pl.BlockSpec(memory_space=pltpu.HBM)
SMEM = pl.BlockSpec(memory_space=pltpu.SMEM)
NN = (((1,), (0,)), ((), ()))
NT = (((1,), (1,)), ((), ()))
TN = (((0,), (0,)), ((), ()))


def shift(block, axis, distance):
    n = lax.axis_size(axis)
    return lax.ppermute(block, axis, [(i, (i + distance) % n) for i in range(n)])


def dot(left, right, dims):
    return lax.dot_general(left, right, dims, preferred_element_type=F32)


def both(left, right, axis):
    return shift(left, axis, 1), shift(right, axis, -1)


def params(mib=26):
    return pltpu.CompilerParams(vmem_limit_bytes=mib * MIB)


def cost(flops, nbytes):
    return pl.CostEstimate(flops=flops, bytes_accessed=nbytes, transcendentals=0)


def sds(*shape, dtype=BF16):
    return jax.ShapeDtypeStruct(shape, dtype)


OFFSETS = (0, -1, 1, -2, 2, -3, 3)


def put_column(pos_ref, out_ref, pieces):
    for k, piece in zip(OFFSETS, pieces):
        out_ref[lax.rem(pos_ref[0] + (k + 8), 8)] = piece[...]


def inputs_kernel(share, pos_ref, *refs):
    tok_pieces, cot_pieces, (far_l, far_r) = refs[:7], refs[7:14], refs[14:16]
    tok_ref, cot_ref, *sends = refs[16:]
    z, dp = pos_ref[0], pos_ref[2]
    opposite = lax.rem(z + 4, 8)
    half = far_l.shape[0] // 2
    for n, (out_ref, pieces) in enumerate(((tok_ref, tok_pieces), (cot_ref, cot_pieces))):
        put_column(pos_ref, out_ref, pieces)
        out_ref[opposite, :half] = far_l[n * half : (n + 1) * half, :]
        out_ref[opposite, half:] = far_r[n * half : (n + 1) * half, :]
        first = pl.multiple_of(lax.rem(z, 4) * share, 16)
        for d, send in zip((1, 2, 3), sends):
            chip = lax.rem(dp + d, 4) * 2 + z // 4
            send[n * share : (n + 1) * share, :] = out_ref[chip, pl.ds(first, share), :]


def blocks_kernel(pos_ref, *refs):
    *pieces, far_l, far_r, out_ref = refs
    put_column(pos_ref, out_ref, pieces)
    opposite = lax.rem(pos_ref[0] + 4, 8)
    half = far_l.shape[0]
    out_ref[opposite, :half] = far_l[...]
    out_ref[opposite, half:] = far_r[...]


def lay_out(pos_ref, tile, own, other):
    core = pos_ref[1]
    height = own.shape[1]
    for chip in range(8):
        base = chip * 2 * height
        tile[pl.ds(pl.multiple_of(base + core * height, 64), height), :] = own[chip]
        tile[pl.ds(pl.multiple_of(base + (1 - core) * height, 64), height), :] = other[chip]


def keep_row(pos_ref, levels_ref, tokens):
    rank = pos_ref[0] * 2 + pos_ref[1]
    return jnp.concatenate(
        [
            jnp.full((1, BLOCK), (levels_ref[b] > rank).astype(F32), F32)
            for b in range(tokens // BLOCK)
        ],
        axis=1,
    )


def own_rows(pos_ref, tile, blk_ref):
    rows = blk_ref.shape[0]
    blk_ref[...] = tile[pl.ds(pl.multiple_of(pos_ref[2] * rows, 64), rows), :]


def fetch(pairs, sem):
    copies = [pltpu.make_async_copy(src, dst, sem.at[n]) for n, (src, dst) in enumerate(pairs)]
    for copy in copies:
        copy.start()
    return copies


def up_kernel(pos_ref, levels_ref, tok, tok_other, w_in, sq_ref, rect_ref, blk_ref, tile, w, sem):
    n_tiles, _, size = w.shape
    tiles = [slice(n * size, (n + 1) * size) for n in range(n_tiles)]
    copies = fetch([(w_in.at[:, part], w.at[n]) for n, part in enumerate(tiles)], sem)
    keep = keep_row(pos_ref, levels_ref, tile.shape[1])
    lay_out(pos_ref, tile, tok, tok_other)
    own_rows(pos_ref, tile, blk_ref)
    for n, part in enumerate(tiles):
        copies[n].wait()
        rect = jnp.maximum(dot(w[n], tile[...], TN), 0.0)
        rect_ref[part, :] = rect
        sq_ref[part, :] = (rect * rect * keep).astype(BF16)


def down_kernel(pos_ref, levels_ref, cot, cot_other, w_out, rect_ref, hid_ref, blk_ref, tile, w, sem):
    n_tiles, size, _ = w.shape
    tiles = [slice(n * size, (n + 1) * size) for n in range(n_tiles)]
    copies = fetch([(w_out.at[part, :], w.at[n]) for n, part in enumerate(tiles)], sem)
    keep = keep_row(pos_ref, levels_ref, tile.shape[1])
    lay_out(pos_ref, tile, cot, cot_other)
    own_rows(pos_ref, tile, blk_ref)
    for n, part in enumerate(tiles):
        copies[n].wait()
        grad = dot(w[n], tile[...], NN)
        hid_ref[part, :] = (grad * 2.0 * rect_ref[part, :] * keep).astype(BF16)


def back_kernel(pos_ref, w_ref, w_other_ref, hid_ref, hid_other_ref, out_ref, w, sem):
    z, core = pos_ref[0], pos_ref[1]
    height = out_ref.shape[1]
    rows = []
    for k in range(8):
        first = lax.rem(z + k, 8) * (2 * height) + core * height
        rows.append(pl.ds(pl.multiple_of(first, 64), height))
    copies = fetch([(w_ref.at[rows[k], :], w.at[k]) for k in range(8)], sem)
    for k in range(8):
        copies[k].wait()
        term = dot(w[k], hid_ref[...], NN) + dot(w_other_ref[rows[k], :], hid_other_ref[...], NN)
        out_ref[k] = term.astype(BF16)


def wgrad_kernel(share, pos_ref, tok_blk, cot_blk, col, col_other, *refs):
    *hidden, out_ref, in_ref, tok_far, cot_far, blk = refs
    core = pos_ref[1]
    per_group = col.shape[1] // 3
    for g in range(3):
        for m in range(2):
            source = slice(g * per_group + m * share, g * per_group + (m + 1) * share)
            ref = blk.at[g, m] if g < 2 else (tok_far, cot_far)[m]
            for chip in range(8):
                first = chip // 4 * (8 * share) + chip % 4 * share
                ref[pl.ds(pl.multiple_of(first + core * (4 * share), 16), share), :] = col[chip, source, :]
                ref[pl.ds(pl.multiple_of(first + (1 - core) * (4 * share), 16), share), :] = col_other[chip, source, :]
    acc_out = acc_in = 0.0
    for g in range(3):
        tok, cot = (tok_blk[...], cot_blk[...]) if g == 0 else (blk[g - 1, 0], blk[g - 1, 1])
        acc_out += dot(hidden[2 * g][...], cot, NT)
        acc_in += dot(tok, hidden[2 * g + 1][...], NT)
    out_ref[...] = acc_out
    in_ref[...] = acc_in


def last_kernel(scale, acc_out, acc_in, tok_far, cot_far, sq_l, sq_r, hid_l, hid_r, out_ref, in_ref):
    half = sq_l.shape[0]
    for n, (sq, hid) in enumerate(((sq_l, hid_l), (sq_r, hid_r))):
        part = slice(n * half, (n + 1) * half)
        out_ref[part, :] = ((acc_out[part, :] + dot(sq[...], cot_far[...], NT)) * scale).astype(BF16)
        in_ref[:, part] = ((acc_in[:, part] + dot(tok_far[...], hid[...], NT)) * scale).astype(BF16)


def plus(a, b):
    return (a.astype(F32) + b.astype(F32)).astype(BF16)


def shards(tokens, cotangent, w_in, w_out, levels):
    z, core, dp = lax.axis_index("z"), lax.axis_index("core"), lax.axis_index("dp")
    pos = jnp.stack([z, core, dp]).astype(jnp.int32)
    w_in, w_out, levels = w_in[0], w_out[0], levels[0]
    d, f = w_in.shape
    t, width = tokens.shape[1:]
    rows = d // 4
    share = rows // 16
    half, cut = f // 2, width // 2
    flops = 2 * t * d * f

    def call(kernel, out_shape, n_scalars, operands, scratch=(), work=0, hbm=(), name=None):
        return pl.pallas_call(
            kernel,
            out_shape=out_shape,
            in_specs=[
                SMEM if n < n_scalars else HBM if n in hbm else VMEM for n in range(len(operands))
            ],
            out_specs=jax.tree.map(lambda _: VMEM, out_shape),
            scratch_shapes=scratch,
            compiler_params=params(),
            cost_estimate=cost(work, work // 256),
            name=name,
        )(*(pltpu.with_memory_space_constraint(x, pltpu.HBM) if n in hbm else x for n, x in enumerate(operands)))

    w_other = shift(w_in, "core", 1)
    tok_ring, cot_ring = [(tokens[0].T,) * 2], [(cotangent[0].T,) * 2]
    for _ in range(3):
        tok_ring.append(both(*tok_ring[-1], "z"))
        cot_ring.append(both(*cot_ring[-1], "z"))
    (tok_l, tok_r), (cot_l, cot_r) = tok_ring[-1], cot_ring[-1]
    far = both(
        jnp.concatenate([tok_l[:cut], cot_l[:cut]]), jnp.concatenate([tok_r[cut:], cot_r[cut:]]), "z"
    )
    far, w_other = lax.optimization_barrier((far, w_other))
    tok_pieces = (tok_ring[0][0], *(p for pair in tok_ring[1:] for p in pair))
    cot_pieces = (cot_ring[0][0], *(p for pair in cot_ring[1:] for p in pair))
    tok, cot, *sends = call(
        functools.partial(inputs_kernel, share),
        (sds(8, width, t), sds(8, width, t)) + (sds(2 * share, t),) * 3,
        1,
        (pos, *tok_pieces, *cot_pieces, *far),
        name="inputs",
    )
    tok_other, cot_other = shift(tok, "core", 1), shift(cot, "core", 1)
    shares = shift(sends[0], "dp", 1), shift(sends[2], "dp", -1), shift(sends[1], "dp", 2)
    size, n_tiles = 256, f // 256
    rect_and_blk = (sds(f, t, dtype=F32), sds(rows, t))
    sq, rect, tok_blk = call(
        up_kernel,
        (sds(f, t), *rect_and_blk),
        2,
        (pos, levels, tok, tok_other, w_in),
        [
            pltpu.VMEM((d, t), BF16),
            pltpu.VMEM((n_tiles, d, size), BF16),
            pltpu.SemaphoreType.DMA((n_tiles,)),
        ],
        2 * flops,
        (4,),
        "up",
    )

    sq_sent, shares = lax.optimization_barrier((sq, shares))
    sq_l, sq_r = both(sq_sent, sq_sent, "dp")
    piece = jnp.concatenate(shares)
    l1, r1 = both(piece, piece, "z")
    cot_other, l1, r1 = lax.optimization_barrier((cot_other, l1, r1))
    hid, cot_blk = call(
        down_kernel,
        (sds(f, t), sds(rows, t)),
        2,
        (pos, levels, cot, cot_other, w_out, rect),
        [
            pltpu.VMEM((d, t), BF16),
            pltpu.VMEM((n_tiles, size, d), BF16),
            pltpu.SemaphoreType.DMA((n_tiles,)),
        ],
        0,
        (4,),
        "down",
    )
    hid_other = shift(hid, "core", 1)
    l2, r2 = both(l1, r1, "z")
    hid_sent, hid_other, sq_l, sq_r = lax.optimization_barrier((hid, hid_other, sq_l, sq_r))
    terms = call(
        back_kernel,
        sds(8, width, t),
        1,
        (pos, w_in, w_other, hid, hid_other),
        [pltpu.VMEM((8, width, f), BF16), pltpu.SemaphoreType.DMA((8,))],
        2 * flops,
        (1,),
        "back",
    )
    hid_l, hid_r = both(hid_sent, hid_sent, "dp")
    l3, r3 = both(l2, r2, "z")
    right, left = both(terms[4, :cut], terms[4, cut:], "z")
    right, left, l3, r3 = lax.optimization_barrier((right, left, l3, r3))
    part = piece.shape[0] // 2
    far = both(l3[:part], r3[part:], "z")
    right, left = both(
        plus(terms[3], jnp.pad(right, ((0, cut), (0, 0)))),
        plus(terms[5], jnp.pad(left, ((cut, 0), (0, 0)))),
        "z",
    )
    right, left, far, hid_l, hid_r = lax.optimization_barrier((right, left, far, hid_l, hid_r))
    sq_ol, sq_or = both(sq_l[:half], sq_r[half:], "dp")
    hid_ol, hid_or = both(hid_l[:half], hid_r[half:], "dp")
    right, left = both(plus(terms[2], right), plus(terms[6], left), "z")
    right, left = lax.optimization_barrier((right, left))
    right, left = both(plus(terms[1], right), plus(terms[7], left), "z")

    blocks = call(
        blocks_kernel,
        sds(8, *piece.shape),
        1,
        (pos, piece, l1, r1, l2, r2, l3, r3, *far),
        name="blocks",
    )
    blocks_other = shift(blocks, "core", 1)
    scale = 1.0 / math.sqrt(t * lax.axis_size("dp"))

    acc_out, acc_in, tok_far, cot_far = call(
        functools.partial(wgrad_kernel, share),
        (sds(f, rows, dtype=F32), sds(rows, f, dtype=F32), sds(rows, t), sds(rows, t)),
        1,
        (pos, tok_blk, cot_blk, blocks, blocks_other, sq, hid, sq_l, hid_l, sq_r, hid_r),
        [pltpu.VMEM((2, 2, rows, t), BF16)],
        flops,
        name="wgrad",
    )
    right, left, acc_out, sq_ol, sq_or = lax.optimization_barrier((right, left, acc_out, sq_ol, sq_or))
    input_sum = (terms[0].astype(F32) + right.astype(F32) + left.astype(F32)).astype(BF16)
    grad_out, grad_in = call(
        functools.partial(last_kernel, scale),
        (sds(f, rows), sds(rows, f)),
        0,
        (acc_out, acc_in, tok_far, cot_far, sq_ol, sq_or, hid_ol, hid_or),
        name="last",
    )
    n_pipe = lax.axis_size("pipe")
    received = lax.ppermute(input_sum, "pipe", [(i, i - 1) for i in range(1, n_pipe)])
    return (received.T[None], grad_in[None], grad_out[None])


def solution(mesh):
    n_pipe, n_dp, n_tensor = mesh.devices.shape
    fine = Mesh(mesh.devices.reshape(n_pipe, n_dp, n_tensor // 2, 2), ("pipe", "dp", "z", "core"))
    tensor = ("z", "core")
    return jax.shard_map(
        shards,
        mesh=fine,
        in_specs=(
            P("pipe", "dp", tensor),
            P("pipe", "dp", tensor),
            P("pipe", None, tensor),
            P("pipe", tensor, None),
            P("pipe", "dp"),
        ),
        out_specs=(P("pipe", "dp", tensor), P("pipe", "dp", tensor), P("pipe", tensor, "dp")),
        check_vma=False,
    )
```

```python
import functools
import math

import jax
import jax.numpy as jnp
from jax import lax
from jax.experimental import pallas as pl
from jax.experimental.pallas import tpu as pltpu
from jax.sharding import Mesh
from jax.sharding import PartitionSpec as P

BLOCK = 128
MIB = 1 << 20
F32 = jnp.float32
BF16 = jnp.bfloat16
VMEM = pl.BlockSpec(memory_space=pltpu.VMEM)
HBM = pl.BlockSpec(memory_space=pltpu.HBM)
SMEM = pl.BlockSpec(memory_space=pltpu.SMEM)
NN = (((1,), (0,)), ((), ()))
NT = (((1,), (1,)), ((), ()))
TN = (((0,), (0,)), ((), ()))


def shift(block, axis, distance):
    n = lax.axis_size(axis)
    return lax.ppermute(block, axis, [(i, (i + distance) % n) for i in range(n)])


def dot(left, right, dims):
    return lax.dot_general(left, right, dims, preferred_element_type=F32)


def both(left, right, axis):
    return shift(left, axis, 1), shift(right, axis, -1)


def params(mib=26):
    return pltpu.CompilerParams(vmem_limit_bytes=mib * MIB)


def cost(flops, nbytes):
    return pl.CostEstimate(flops=flops, bytes_accessed=nbytes, transcendentals=0)


def sds(*shape, dtype=BF16):
    return jax.ShapeDtypeStruct(shape, dtype)


OFFSETS = (0, -1, 1, -2, 2, -3, 3)


def put_column(pos_ref, out_ref, pieces):
    for k, piece in zip(OFFSETS, pieces):
        out_ref[lax.rem(pos_ref[0] + (k + 8), 8)] = piece[...]


def inputs_kernel(share, pos_ref, *refs):
    tok_pieces, cot_pieces, (far_l, far_r) = refs[:7], refs[7:14], refs[14:16]
    tok_ref, cot_ref, *sends = refs[16:]
    z, dp = pos_ref[0], pos_ref[2]
    opposite = lax.rem(z + 4, 8)
    half = far_l.shape[0] // 2
    for n, (out_ref, pieces) in enumerate(((tok_ref, tok_pieces), (cot_ref, cot_pieces))):
        put_column(pos_ref, out_ref, pieces)
        out_ref[opposite, :half] = far_l[n * half : (n + 1) * half, :]
        out_ref[opposite, half:] = far_r[n * half : (n + 1) * half, :]
        first = pl.multiple_of(lax.rem(z, 4) * share, 16)
        for d, send in zip((1, 2, 3), sends):
            chip = lax.rem(dp + d, 4) * 2 + z // 4
            send[n * share : (n + 1) * share, :] = out_ref[chip, pl.ds(first, share), :]


def blocks_kernel(pos_ref, *refs):
    *pieces, far_l, far_r, out_ref = refs
    put_column(pos_ref, out_ref, pieces)
    opposite = lax.rem(pos_ref[0] + 4, 8)
    half = far_l.shape[0]
    out_ref[opposite, :half] = far_l[...]
    out_ref[opposite, half:] = far_r[...]


def lay_out(pos_ref, tile, own, other):
    core = pos_ref[1]
    height = own.shape[1]
    for chip in range(8):
        base = chip * 2 * height
        tile[pl.ds(pl.multiple_of(base + core * height, 64), height), :] = own[chip]
        tile[pl.ds(pl.multiple_of(base + (1 - core) * height, 64), height), :] = other[chip]


def keep_row(pos_ref, levels_ref, tokens):
    rank = pos_ref[0] * 2 + pos_ref[1]
    return jnp.concatenate(
        [
            jnp.full((1, BLOCK), (levels_ref[b] > rank).astype(F32), F32)
            for b in range(tokens // BLOCK)
        ],
        axis=1,
    )


def own_rows(pos_ref, tile, blk_ref):
    rows = blk_ref.shape[0]
    blk_ref[...] = tile[pl.ds(pl.multiple_of(pos_ref[2] * rows, 64), rows), :]


def fetch(pairs, sem):
    copies = [pltpu.make_async_copy(src, dst, sem.at[n]) for n, (src, dst) in enumerate(pairs)]
    for copy in copies:
        copy.start()
    return copies


def hidden_kernel(
    pos_ref, levels_ref, tok, tok_other, cot, cot_other, w_in, w_out, hid_ref, bundle_ref, tok_ref, cot_ref, tile, cot_tile, rect_ref, win, wout, sem
):
    n_tiles, size = wout.shape[:2]
    tiles = [slice(n * size, (n + 1) * size) for n in range(n_tiles)]
    copies = fetch(
        [(w_in.at[:, part], win.at[n]) for n, part in enumerate(tiles)]
        + [(w_out.at[part, :], wout.at[n]) for n, part in enumerate(tiles)],
        sem,
    )
    keep = keep_row(pos_ref, levels_ref, tile.shape[1])
    half = hid_ref.shape[0] // 2

    def put(n, block, kind):
        for m in range(2):
            low, high = max(n * size, m * half), min((n + 1) * size, (m + 1) * half)
            if low < high:
                start = (2 * m + kind) * half + low - m * half
                bundle_ref[start : start + high - low, :] = block[low - n * size : high - n * size]

    lay_out(pos_ref, tile, tok, tok_other)
    own_rows(pos_ref, tile, tok_ref)
    for n, part in enumerate(tiles):
        copies[n].wait()
        rect = jnp.maximum(dot(win[n], tile[...], TN), 0.0)
        rect_ref[part, :] = rect
        put(n, (rect * rect * keep).astype(BF16), 0)
    lay_out(pos_ref, cot_tile, cot, cot_other)
    own_rows(pos_ref, cot_tile, cot_ref)
    for n, part in enumerate(tiles):
        copies[n_tiles + n].wait()
        grad = dot(wout[n], cot_tile[...], NN)
        hid = (grad * 2.0 * rect_ref[part, :] * keep).astype(BF16)
        hid_ref[part, :] = hid
        put(n, hid, 1)


def back_kernel(pos_ref, w_ref, w_other_ref, hid_ref, hid_other_ref, out_ref, w, acc, sem):
    z, core = pos_ref[0], pos_ref[1]
    height = out_ref.shape[1]
    rows = []
    for k in range(8):
        first = lax.rem(z + k, 8) * (2 * height) + core * height
        rows.append(pl.ds(pl.multiple_of(first, 64), height))
    copies = fetch([(w_ref.at[rows[k], :], w.at[k]) for k in range(8)], sem)
    for k in range(8):
        acc[k] = dot(w_other_ref[rows[k], :], hid_other_ref[...], NN)
    for k in range(8):
        copies[k].wait()
        out_ref[k] = (acc[k] + dot(w[k], hid_ref[...], NN)).astype(BF16)


def wgrad_kernel(share, pos_ref, tok_blk, cot_blk, col, col_other, *refs):
    *bundles, out_ref, in_ref, tok_far, cot_far, blk = refs
    core = pos_ref[1]
    per_group = col.shape[1] // 3
    for g in range(3):
        for m in range(2):
            source = slice(g * per_group + m * share, g * per_group + (m + 1) * share)
            ref = blk.at[g, m] if g < 2 else (tok_far, cot_far)[m]
            for chip in range(8):
                first = chip // 4 * (8 * share) + chip % 4 * share
                ref[pl.ds(pl.multiple_of(first + core * (4 * share), 16), share), :] = col[chip, source, :]
                ref[pl.ds(pl.multiple_of(first + (1 - core) * (4 * share), 16), share), :] = col_other[chip, source, :]
    half = out_ref.shape[0] // 2
    for n in range(2):
        part = slice(n * half, (n + 1) * half)
        acc_out = acc_in = 0.0
        for g, bundle in enumerate(bundles):
            tok, cot = (tok_blk[...], cot_blk[...]) if g == 0 else (blk[g - 1, 0], blk[g - 1, 1])
            acc_out += dot(bundle[2 * n * half : (2 * n + 1) * half, :], cot, NT)
            acc_in += dot(tok, bundle[(2 * n + 1) * half : (2 * n + 2) * half, :], NT)
        out_ref[part, :] = acc_out
        in_ref[:, part] = acc_in


def last_kernel(scale, acc_out, acc_in, tok_far, cot_far, far_a, far_b, out_ref, in_ref):
    half = far_a.shape[0] // 2
    for n, bundle in enumerate((far_a, far_b)):
        part = slice(n * half, (n + 1) * half)
        out_ref[part, :] = ((acc_out[part, :] + dot(bundle[:half, :], cot_far[...], NT)) * scale).astype(BF16)
        in_ref[:, part] = ((acc_in[:, part] + dot(tok_far[...], bundle[half:, :], NT)) * scale).astype(BF16)


def plus(a, b):
    return (a.astype(F32) + b.astype(F32)).astype(BF16)


def shards(tokens, cotangent, w_in, w_out, levels):
    z, core, dp = lax.axis_index("z"), lax.axis_index("core"), lax.axis_index("dp")
    pos = jnp.stack([z, core, dp]).astype(jnp.int32)
    w_in, w_out, levels = w_in[0], w_out[0], levels[0]
    d, f = w_in.shape
    t, width = tokens.shape[1:]
    rows = d // 4
    share = rows // 16
    half, cut = f // 2, width // 2
    flops = 2 * t * d * f

    def call(kernel, out_shape, n_scalars, operands, scratch=(), work=0, hbm=(), name=None):
        return pl.pallas_call(
            kernel,
            out_shape=out_shape,
            in_specs=[
                SMEM if n < n_scalars else HBM if n in hbm else VMEM for n in range(len(operands))
            ],
            out_specs=jax.tree.map(lambda _: VMEM, out_shape),
            scratch_shapes=scratch,
            compiler_params=params(),
            cost_estimate=cost(work, work // 256),
            name=name,
        )(*(pltpu.with_memory_space_constraint(x, pltpu.HBM) if n in hbm else x for n, x in enumerate(operands)))

    w_other = shift(w_in, "core", 1)
    tok_ring, cot_ring = [(tokens[0].T,) * 2], [(cotangent[0].T,) * 2]
    for _ in range(3):
        tok_ring.append(both(*tok_ring[-1], "z"))
        cot_ring.append(both(*cot_ring[-1], "z"))
    (tok_l, tok_r), (cot_l, cot_r) = tok_ring[-1], cot_ring[-1]
    far = both(
        jnp.concatenate([tok_l[:cut], cot_l[:cut]]), jnp.concatenate([tok_r[cut:], cot_r[cut:]]), "z"
    )
    far, w_other = lax.optimization_barrier((far, w_other))
    tok_pieces = (tok_ring[0][0], *(p for pair in tok_ring[1:] for p in pair))
    cot_pieces = (cot_ring[0][0], *(p for pair in cot_ring[1:] for p in pair))
    tok, cot, *sends = call(
        functools.partial(inputs_kernel, share),
        (sds(8, width, t), sds(8, width, t)) + (sds(2 * share, t),) * 3,
        1,
        (pos, *tok_pieces, *cot_pieces, *far),
        name="inputs",
    )
    tok_other, cot_other = shift(tok, "core", 1), shift(cot, "core", 1)
    shares = shift(sends[0], "dp", 1), shift(sends[2], "dp", -1), shift(sends[1], "dp", 2)
    piece = jnp.concatenate(shares)
    cot_other, piece = lax.optimization_barrier((cot_other, piece))
    size = 256
    hid, bundle, tok_blk, cot_blk = call(
        hidden_kernel,
        (sds(f, t), sds(2 * f, t), sds(rows, t), sds(rows, t)),
        2,
        (pos, levels, tok, tok_other, cot, cot_other, w_in, w_out),
        [
            pltpu.VMEM((d, t), BF16),
            pltpu.VMEM((d, t), BF16),
            pltpu.VMEM((f, t), F32),
            pltpu.VMEM((f // size, d, size), BF16),
            pltpu.VMEM((f // size, size, d), BF16),
            pltpu.SemaphoreType.DMA((2 * f // size,)),
        ],
        hbm=(6, 7),
        name="hidden",
    )

    hid_other = shift(hid, "core", 1)
    bundle_l, bundle_r = both(bundle, bundle, "dp")
    l1, r1 = both(piece, piece, "z")
    terms = call(
        back_kernel,
        sds(8, width, t),
        1,
        (pos, w_in, w_other, hid, hid_other),
        [pltpu.VMEM((8, width, f), BF16), pltpu.VMEM((8, width, t), F32), pltpu.SemaphoreType.DMA((8,))],
        2 * flops,
        (1,),
        name="back",
    )
    l1, r1, terms = lax.optimization_barrier((l1, r1, terms))
    l2, r2 = both(l1, r1, "z")
    l3, r3 = both(l2, r2, "z")
    part = piece.shape[0] // 2
    far = both(l3[:part], r3[part:], "z")
    right, left = both(terms[4, :cut], terms[4, cut:], "z")
    right, left = lax.optimization_barrier((right, left))
    right, left = both(
        plus(terms[3], jnp.pad(right, ((0, cut), (0, 0)))),
        plus(terms[5], jnp.pad(left, ((cut, 0), (0, 0)))),
        "z",
    )
    right, left, far, bundle_l, bundle_r = lax.optimization_barrier((right, left, far, bundle_l, bundle_r))
    far_a, far_b = both(bundle_l[:f], bundle_r[f:], "dp")
    right, left = both(plus(terms[2], right), plus(terms[6], left), "z")
    right, left = lax.optimization_barrier((right, left))
    right, left = both(plus(terms[1], right), plus(terms[7], left), "z")

    blocks = call(
        blocks_kernel,
        sds(8, *piece.shape),
        1,
        (pos, piece, l1, r1, l2, r2, l3, r3, *far),
        name="blocks",
    )
    blocks_other = shift(blocks, "core", 1)
    scale = 1.0 / math.sqrt(t * lax.axis_size("dp"))

    acc_out, acc_in, tok_far, cot_far = call(
        functools.partial(wgrad_kernel, share),
        (sds(f, rows, dtype=F32), sds(rows, f, dtype=F32), sds(rows, t), sds(rows, t)),
        1,
        (pos, tok_blk, cot_blk, blocks, blocks_other, bundle, bundle_l, bundle_r),
        [pltpu.VMEM((2, 2, rows, t), BF16)],
        flops,
        name="wgrad",
    )
    right, left, acc_out = lax.optimization_barrier((right, left, acc_out))
    input_sum = (terms[0].astype(F32) + right.astype(F32) + left.astype(F32)).astype(BF16)
    grad_out, grad_in = call(
        functools.partial(last_kernel, scale),
        (sds(f, rows), sds(rows, f)),
        0,
        (acc_out, acc_in, tok_far, cot_far, far_a, far_b),
        name="last",
    )
    n_pipe = lax.axis_size("pipe")
    received = lax.ppermute(input_sum, "pipe", [(i, i - 1) for i in range(1, n_pipe)])
    return (received.T[None], grad_in[None], grad_out[None])


def solution(mesh):
    n_pipe, n_dp, n_tensor = mesh.devices.shape
    fine = Mesh(mesh.devices.reshape(n_pipe, n_dp, n_tensor // 2, 2), ("pipe", "dp", "z", "core"))
    tensor = ("z", "core")
    return jax.shard_map(
        shards,
        mesh=fine,
        in_specs=(
            P("pipe", "dp", tensor),
            P("pipe", "dp", tensor),
            P("pipe", None, tensor),
            P("pipe", tensor, None),
            P("pipe", "dp"),
        ),
        out_specs=(P("pipe", "dp", tensor), P("pipe", "dp", tensor), P("pipe", tensor, "dp")),
        check_vma=False,
    )
```

```python
import functools
import math

import jax
import jax.numpy as jnp
from jax import lax
from jax.experimental import pallas as pl
from jax.experimental.pallas import tpu as pltpu
from jax.sharding import Mesh
from jax.sharding import PartitionSpec as P

BLOCK = 128
MIB = 1 << 20
F32 = jnp.float32
BF16 = jnp.bfloat16
VMEM = pl.BlockSpec(memory_space=pltpu.VMEM)
HBM = pl.BlockSpec(memory_space=pltpu.HBM)
SMEM = pl.BlockSpec(memory_space=pltpu.SMEM)
NN = (((1,), (0,)), ((), ()))
NT = (((1,), (1,)), ((), ()))
TN = (((0,), (0,)), ((), ()))


def shift(block, axis, distance):
    n = lax.axis_size(axis)
    return lax.ppermute(block, axis, [(i, (i + distance) % n) for i in range(n)])


def dot(left, right, dims):
    return lax.dot_general(left, right, dims, preferred_element_type=F32)


def both(left, right, axis):
    return shift(left, axis, 1), shift(right, axis, -1)


def params(mib=26):
    return pltpu.CompilerParams(vmem_limit_bytes=mib * MIB)


def cost(flops, nbytes):
    return pl.CostEstimate(flops=flops, bytes_accessed=nbytes, transcendentals=0)


def sds(*shape, dtype=BF16):
    return jax.ShapeDtypeStruct(shape, dtype)


OFFSETS = (0, -1, 1, -2, 2, -3, 3)


def put_column(pos_ref, out_ref, pieces):
    for k, piece in zip(OFFSETS, pieces):
        out_ref[lax.rem(pos_ref[0] + (k + 8), 8)] = piece[...]


def inputs_kernel(share, pos_ref, *refs):
    tok_pieces, cot_pieces, (far_l, far_r) = refs[:7], refs[7:14], refs[14:16]
    tok_ref, cot_ref, *sends = refs[16:]
    z, dp = pos_ref[0], pos_ref[2]
    opposite = lax.rem(z + 4, 8)
    half = far_l.shape[0] // 2
    for n, (out_ref, pieces) in enumerate(((tok_ref, tok_pieces), (cot_ref, cot_pieces))):
        put_column(pos_ref, out_ref, pieces)
        out_ref[opposite, :half] = far_l[n * half : (n + 1) * half, :]
        out_ref[opposite, half:] = far_r[n * half : (n + 1) * half, :]
        first = pl.multiple_of(lax.rem(z, 4) * share, 16)
        for d, send in zip((1, 2, 3), sends):
            chip = lax.rem(dp + d, 4) * 2 + z // 4
            send[n * share : (n + 1) * share, :] = out_ref[chip, pl.ds(first, share), :]


def blocks_kernel(pos_ref, *refs):
    *pieces, far_l, far_r, out_ref = refs
    put_column(pos_ref, out_ref, pieces)
    opposite = lax.rem(pos_ref[0] + 4, 8)
    half = far_l.shape[0]
    out_ref[opposite, :half] = far_l[...]
    out_ref[opposite, half:] = far_r[...]


def lay_out(pos_ref, tile, own, other):
    core = pos_ref[1]
    height = own.shape[1]
    for chip in range(8):
        base = chip * 2 * height
        tile[pl.ds(pl.multiple_of(base + core * height, 64), height), :] = own[chip]
        tile[pl.ds(pl.multiple_of(base + (1 - core) * height, 64), height), :] = other[chip]


def keep_row(pos_ref, levels_ref, tokens):
    rank = pos_ref[0] * 2 + pos_ref[1]
    return jnp.concatenate(
        [
            jnp.full((1, BLOCK), (levels_ref[b] > rank).astype(F32), F32)
            for b in range(tokens // BLOCK)
        ],
        axis=1,
    )


def own_rows(pos_ref, tile, blk_ref):
    rows = blk_ref.shape[0]
    blk_ref[...] = tile[pl.ds(pl.multiple_of(pos_ref[2] * rows, 64), rows), :]


def fetch(pairs, sem):
    copies = [pltpu.make_async_copy(src, dst, sem.at[n]) for n, (src, dst) in enumerate(pairs)]
    for copy in copies:
        copy.start()
    return copies


def hidden_kernel(
    pos_ref, levels_ref, tok, tok_other, cot, cot_other, w_in, w_out, hid_ref, bundle_ref, tok_ref, cot_ref, tile, cot_tile, rect_ref, win, wout, sem
):
    n_tiles, size = wout.shape[:2]
    tiles = [slice(n * size, (n + 1) * size) for n in range(n_tiles)]
    copies = fetch(
        [(w_in.at[:, part], win.at[n]) for n, part in enumerate(tiles)]
        + [(w_out.at[part, :], wout.at[n]) for n, part in enumerate(tiles)],
        sem,
    )
    keep = keep_row(pos_ref, levels_ref, tile.shape[1])
    half = hid_ref.shape[0] // 2

    def put(n, block, kind):
        for m in range(2):
            low, high = max(n * size, m * half), min((n + 1) * size, (m + 1) * half)
            if low < high:
                start = (2 * m + kind) * half + low - m * half
                bundle_ref[start : start + high - low, :] = block[low - n * size : high - n * size]

    lay_out(pos_ref, tile, tok, tok_other)
    own_rows(pos_ref, tile, tok_ref)
    for n, part in enumerate(tiles):
        copies[n].wait()
        rect = jnp.maximum(dot(win[n], tile[...], TN), 0.0)
        rect_ref[part, :] = rect
        put(n, (rect * rect * keep).astype(BF16), 0)
    lay_out(pos_ref, cot_tile, cot, cot_other)
    own_rows(pos_ref, cot_tile, cot_ref)
    for n, part in enumerate(tiles):
        copies[n_tiles + n].wait()
        grad = dot(wout[n], cot_tile[...], NN)
        hid = (grad * 2.0 * rect_ref[part, :] * keep).astype(BF16)
        hid_ref[part, :] = hid
        put(n, hid, 1)


def back_kernel(pos_ref, w_ref, w_other_ref, hid_ref, hid_other_ref, out_ref, w, sem):
    z, core = pos_ref[0], pos_ref[1]
    height = out_ref.shape[1]
    rows = []
    for k in range(8):
        first = lax.rem(z + k, 8) * (2 * height) + core * height
        rows.append(pl.ds(pl.multiple_of(first, 64), height))
    copies = fetch([(w_ref.at[rows[k], :], w.at[k]) for k in range(8)], sem)
    for k in range(8):
        copies[k].wait()
        term = dot(w[k], hid_ref[...], NN) + dot(w_other_ref[rows[k], :], hid_other_ref[...], NN)
        out_ref[k] = term.astype(BF16)


def wgrad_kernel(share, pos_ref, tok_blk, cot_blk, col, col_other, *refs):
    *bundles, out_ref, in_ref, tok_far, cot_far, blk = refs
    core = pos_ref[1]
    per_group = col.shape[1] // 3
    for g in range(3):
        for m in range(2):
            source = slice(g * per_group + m * share, g * per_group + (m + 1) * share)
            ref = blk.at[g, m] if g < 2 else (tok_far, cot_far)[m]
            for chip in range(8):
                first = chip // 4 * (8 * share) + chip % 4 * share
                ref[pl.ds(pl.multiple_of(first + core * (4 * share), 16), share), :] = col[chip, source, :]
                ref[pl.ds(pl.multiple_of(first + (1 - core) * (4 * share), 16), share), :] = col_other[chip, source, :]
    half = out_ref.shape[0] // 2
    for n in range(2):
        part = slice(n * half, (n + 1) * half)
        acc_out = acc_in = 0.0
        for g, bundle in enumerate(bundles):
            tok, cot = (tok_blk[...], cot_blk[...]) if g == 0 else (blk[g - 1, 0], blk[g - 1, 1])
            acc_out += dot(bundle[2 * n * half : (2 * n + 1) * half, :], cot, NT)
            acc_in += dot(tok, bundle[(2 * n + 1) * half : (2 * n + 2) * half, :], NT)
        out_ref[part, :] = acc_out
        in_ref[:, part] = acc_in


def last_kernel(scale, acc_out, acc_in, tok_far, cot_far, far_a, far_b, out_ref, in_ref):
    half = far_a.shape[0] // 2
    for n, bundle in enumerate((far_a, far_b)):
        part = slice(n * half, (n + 1) * half)
        out_ref[part, :] = ((acc_out[part, :] + dot(bundle[:half, :], cot_far[...], NT)) * scale).astype(BF16)
        in_ref[:, part] = ((acc_in[:, part] + dot(tok_far[...], bundle[half:, :], NT)) * scale).astype(BF16)


def to_previous(block, step):
    n_pipe, n_z = lax.axis_size("pipe"), lax.axis_size("z")
    route = [
        (p * n_z + z, (p - 1) * n_z + (z + step) % n_z) for p in range(1, n_pipe) for z in range(n_z)
    ]
    return lax.ppermute(block, ("pipe", "z"), route)


def plus(a, b):
    return (a.astype(F32) + b.astype(F32)).astype(BF16)


def shards(tokens, cotangent, w_in, w_out, levels):
    z, core, dp = lax.axis_index("z"), lax.axis_index("core"), lax.axis_index("dp")
    pos = jnp.stack([z, core, dp]).astype(jnp.int32)
    w_in, w_out, levels = w_in[0], w_out[0], levels[0]
    d, f = w_in.shape
    t, width = tokens.shape[1:]
    rows = d // 4
    share = rows // 16
    half, cut = f // 2, width // 2
    flops = 2 * t * d * f

    def call(kernel, out_shape, n_scalars, operands, scratch=(), work=0, hbm=(), name=None):
        return pl.pallas_call(
            kernel,
            out_shape=out_shape,
            in_specs=[
                SMEM if n < n_scalars else HBM if n in hbm else VMEM for n in range(len(operands))
            ],
            out_specs=jax.tree.map(lambda _: VMEM, out_shape),
            scratch_shapes=scratch,
            compiler_params=params(),
            cost_estimate=cost(work, work // 256),
            name=name,
        )(*(pltpu.with_memory_space_constraint(x, pltpu.HBM) if n in hbm else x for n, x in enumerate(operands)))

    w_other = shift(w_in, "core", 1)
    tok_ring, cot_ring = [(tokens[0].T,) * 2], [(cotangent[0].T,) * 2]
    for _ in range(3):
        tok_ring.append(both(*tok_ring[-1], "z"))
        cot_ring.append(both(*cot_ring[-1], "z"))
    (tok_l, tok_r), (cot_l, cot_r) = tok_ring[-1], cot_ring[-1]
    far = both(
        jnp.concatenate([tok_l[:cut], cot_l[:cut]]), jnp.concatenate([tok_r[cut:], cot_r[cut:]]), "z"
    )
    far, w_other = lax.optimization_barrier((far, w_other))
    tok_pieces = (tok_ring[0][0], *(p for pair in tok_ring[1:] for p in pair))
    cot_pieces = (cot_ring[0][0], *(p for pair in cot_ring[1:] for p in pair))
    tok, cot, *sends = call(
        functools.partial(inputs_kernel, share),
        (sds(8, width, t), sds(8, width, t)) + (sds(2 * share, t),) * 3,
        1,
        (pos, *tok_pieces, *cot_pieces, *far),
        name="inputs",
    )
    tok_other, cot_other = shift(tok, "core", 1), shift(cot, "core", 1)
    shares = shift(sends[0], "dp", 1), shift(sends[2], "dp", -1), shift(sends[1], "dp", 2)
    piece = jnp.concatenate(shares)
    cot_other, piece = lax.optimization_barrier((cot_other, piece))
    size = 256
    hid, bundle, tok_blk, cot_blk = call(
        hidden_kernel,
        (sds(f, t), sds(2 * f, t), sds(rows, t), sds(rows, t)),
        2,
        (pos, levels, tok, tok_other, cot, cot_other, w_in, w_out),
        [
            pltpu.VMEM((d, t), BF16),
            pltpu.VMEM((d, t), BF16),
            pltpu.VMEM((f, t), F32),
            pltpu.VMEM((f // size, d, size), BF16),
            pltpu.VMEM((f // size, size, d), BF16),
            pltpu.SemaphoreType.DMA((2 * f // size,)),
        ],
        hbm=(6, 7),
        name="hidden",
    )

    hid_other = shift(hid, "core", 1)
    bundle_l, bundle_r = both(bundle, bundle, "dp")
    l1, r1 = both(piece, piece, "z")
    terms = call(
        back_kernel,
        sds(8, width, t),
        1,
        (pos, w_in, w_other, hid, hid_other),
        [pltpu.VMEM((8, width, f), BF16), pltpu.SemaphoreType.DMA((8,))],
        2 * flops,
        (1,),
        name="back",
    )
    l1, r1, hid_other = lax.optimization_barrier((l1, r1, hid_other))
    l2, r2 = both(l1, r1, "z")
    l2, r2, terms = lax.optimization_barrier((l2, r2, terms))
    l3, r3 = both(l2, r2, "z")
    part = piece.shape[0] // 2
    far = both(l3[:part], r3[part:], "z")
    right, left = both(
        jnp.concatenate([terms[4, :cut], terms[0, :cut]]), jnp.concatenate([terms[4, cut:], terms[0, cut:]]), "z"
    )
    right, left = lax.optimization_barrier((right, left))
    low = jnp.pad(right[cut:], ((0, cut), (0, 0)))
    high = jnp.pad(left[cut:], ((cut, 0), (0, 0)))
    right, left = both(
        plus(terms[3], jnp.pad(right[:cut], ((0, cut), (0, 0)))),
        plus(terms[5], jnp.pad(left[:cut], ((cut, 0), (0, 0)))),
        "z",
    )
    right, left, far, bundle_l, bundle_r = lax.optimization_barrier((right, left, far, bundle_l, bundle_r))
    far_a, far_b = both(bundle_l[:f], bundle_r[f:], "dp")
    right, left = both(plus(terms[2], right), plus(terms[6], left), "z")
    right, left = lax.optimization_barrier((right, left))
    right = to_previous(plus(terms[1], right.astype(F32) + high.astype(F32)), 1)
    left = to_previous(plus(terms[7], left.astype(F32) + low.astype(F32)), -1)

    blocks = call(
        blocks_kernel,
        sds(8, *piece.shape),
        1,
        (pos, piece, l1, r1, l2, r2, l3, r3, *far),
        name="blocks",
    )
    blocks_other = shift(blocks, "core", 1)
    scale = 1.0 / math.sqrt(t * lax.axis_size("dp"))

    acc_out, acc_in, tok_far, cot_far = call(
        functools.partial(wgrad_kernel, share),
        (sds(f, rows, dtype=F32), sds(rows, f, dtype=F32), sds(rows, t), sds(rows, t)),
        1,
        (pos, tok_blk, cot_blk, blocks, blocks_other, bundle, bundle_l, bundle_r),
        [pltpu.VMEM((2, 2, rows, t), BF16)],
        flops,
        name="wgrad",
    )
    right, left, acc_out = lax.optimization_barrier((right, left, acc_out))
    received = plus(right, left)
    grad_out, grad_in = call(
        functools.partial(last_kernel, scale),
        (sds(f, rows), sds(rows, f)),
        0,
        (acc_out, acc_in, tok_far, cot_far, far_a, far_b),
        name="last",
    )
    return (received.T[None], grad_in[None], grad_out[None])


def solution(mesh):
    n_pipe, n_dp, n_tensor = mesh.devices.shape
    fine = Mesh(mesh.devices.reshape(n_pipe, n_dp, n_tensor // 2, 2), ("pipe", "dp", "z", "core"))
    tensor = ("z", "core")
    return jax.shard_map(
        shards,
        mesh=fine,
        in_specs=(
            P("pipe", "dp", tensor),
            P("pipe", "dp", tensor),
            P("pipe", None, tensor),
            P("pipe", tensor, None),
            P("pipe", "dp"),
        ),
        out_specs=(P("pipe", "dp", tensor), P("pipe", "dp", tensor), P("pipe", tensor, "dp")),
        check_vma=False,
    )
```

```python
import functools
import math

import jax
import jax.numpy as jnp
from jax import lax
from jax.experimental import pallas as pl
from jax.experimental.pallas import tpu as pltpu
from jax.sharding import Mesh
from jax.sharding import PartitionSpec as P

BLOCK = 128
MIB = 1 << 20
F32 = jnp.float32
BF16 = jnp.bfloat16
VMEM = pl.BlockSpec(memory_space=pltpu.VMEM)
HBM = pl.BlockSpec(memory_space=pltpu.HBM)
SMEM = pl.BlockSpec(memory_space=pltpu.SMEM)
NN = (((1,), (0,)), ((), ()))
NT = (((1,), (1,)), ((), ()))
TN = (((0,), (0,)), ((), ()))


def shift(block, axis, distance):
    n = lax.axis_size(axis)
    return lax.ppermute(block, axis, [(i, (i + distance) % n) for i in range(n)])


def dot(left, right, dims):
    return lax.dot_general(left, right, dims, preferred_element_type=F32)


def both(left, right, axis):
    return shift(left, axis, 1), shift(right, axis, -1)


def params(mib=26):
    return pltpu.CompilerParams(vmem_limit_bytes=mib * MIB)


def cost(flops, nbytes):
    return pl.CostEstimate(flops=flops, bytes_accessed=nbytes, transcendentals=0)


def sds(*shape, dtype=BF16):
    return jax.ShapeDtypeStruct(shape, dtype)


OFFSETS = (0, -1, 1, -2, 2, -3, 3)


def put_column(pos_ref, out_ref, pieces):
    for k, piece in zip(OFFSETS, pieces):
        out_ref[lax.rem(pos_ref[0] + (k + 8), 8)] = piece[...]


def inputs_kernel(share, pos_ref, *refs):
    tok_pieces, cot_pieces, (far_l, far_r) = refs[:7], refs[7:14], refs[14:16]
    both_ref, *sends = refs[16:]
    z, dp = pos_ref[0], pos_ref[2]
    opposite = lax.rem(z + 4, 8)
    half = far_l.shape[0] // 2
    for n, pieces in enumerate((tok_pieces, cot_pieces)):
        out_ref = both_ref.at[n]
        put_column(pos_ref, out_ref, pieces)
        out_ref[opposite, :half] = far_l[n * half : (n + 1) * half, :]
        out_ref[opposite, half:] = far_r[n * half : (n + 1) * half, :]
        first = pl.multiple_of(lax.rem(z, 4) * share, 16)
        for d, send in zip((1, 2, 3), sends):
            chip = lax.rem(dp + d, 4) * 2 + z // 4
            send[n * share : (n + 1) * share, :] = out_ref[chip, pl.ds(first, share), :]


def blocks_kernel(pos_ref, *refs):
    *pieces, far_l, far_r, out_ref = refs
    put_column(pos_ref, out_ref, pieces)
    opposite = lax.rem(pos_ref[0] + 4, 8)
    half = far_l.shape[0]
    out_ref[opposite, :half] = far_l[...]
    out_ref[opposite, half:] = far_r[...]


def lay_out(pos_ref, tile, own, other):
    core = pos_ref[1]
    height = own.shape[1]
    for chip in range(8):
        base = chip * 2 * height
        tile[pl.ds(pl.multiple_of(base + core * height, 64), height), :] = own[chip]
        tile[pl.ds(pl.multiple_of(base + (1 - core) * height, 64), height), :] = other[chip]


def keep_row(pos_ref, levels_ref, tokens):
    rank = pos_ref[0] * 2 + pos_ref[1]
    return jnp.concatenate(
        [
            jnp.full((1, BLOCK), (levels_ref[b] > rank).astype(F32), F32)
            for b in range(tokens // BLOCK)
        ],
        axis=1,
    )


def own_rows(pos_ref, tile, blk_ref):
    rows = blk_ref.shape[0]
    blk_ref[...] = tile[pl.ds(pl.multiple_of(pos_ref[2] * rows, 64), rows), :]


def fetch(pairs, sem):
    copies = [pltpu.make_async_copy(src, dst, sem.at[n]) for n, (src, dst) in enumerate(pairs)]
    for copy in copies:
        copy.start()
    return copies


def hidden_kernel(
    pos_ref, levels_ref, own, other, w_in, w_out, hid_ref, bundle_ref, tok_ref, cot_ref, tile, cot_tile, rect_ref, win, wout, sem
):
    n_tiles, size = wout.shape[:2]
    tiles = [slice(n * size, (n + 1) * size) for n in range(n_tiles)]
    copies = fetch(
        [(w_in.at[:, part], win.at[n]) for n, part in enumerate(tiles)]
        + [(w_out.at[part, :], wout.at[n]) for n, part in enumerate(tiles)],
        sem,
    )
    keep = keep_row(pos_ref, levels_ref, tile.shape[1])
    half = hid_ref.shape[0] // 2

    def put(n, block, kind):
        for m in range(2):
            low, high = max(n * size, m * half), min((n + 1) * size, (m + 1) * half)
            if low < high:
                start = (2 * m + kind) * half + low - m * half
                bundle_ref[start : start + high - low, :] = block[low - n * size : high - n * size]

    lay_out(pos_ref, tile, own.at[0], other.at[0])
    own_rows(pos_ref, tile, tok_ref)
    for n, part in enumerate(tiles):
        copies[n].wait()
        rect = jnp.maximum(dot(win[n], tile[...], TN), 0.0)
        rect_ref[part, :] = rect
        put(n, (rect * rect * keep).astype(BF16), 0)
    lay_out(pos_ref, cot_tile, own.at[1], other.at[1])
    own_rows(pos_ref, cot_tile, cot_ref)
    for n, part in enumerate(tiles):
        copies[n_tiles + n].wait()
        grad = dot(wout[n], cot_tile[...], NN)
        hid = (grad * 2.0 * rect_ref[part, :] * keep).astype(BF16)
        hid_ref[part, :] = hid
        put(n, hid, 1)


def back_kernel(pos_ref, w_ref, w_other_ref, hid_ref, hid_other_ref, out_ref, w, sem):
    z, core = pos_ref[0], pos_ref[1]
    height = out_ref.shape[1]
    rows = []
    for k in range(8):
        first = lax.rem(z + k, 8) * (2 * height) + core * height
        rows.append(pl.ds(pl.multiple_of(first, 64), height))
    copies = fetch([(w_ref.at[rows[k], :], w.at[k]) for k in range(8)], sem)
    for k in range(8):
        copies[k].wait()
        term = dot(w[k], hid_ref[...], NN) + dot(w_other_ref[rows[k], :], hid_other_ref[...], NN)
        out_ref[k] = term.astype(BF16)


def wgrad_kernel(share, pos_ref, tok_blk, cot_blk, col, col_other, *refs):
    *bundles, out_ref, in_ref, tok_far, cot_far, blk = refs
    core = pos_ref[1]
    per_group = col.shape[1] // 3
    for g in range(3):
        for m in range(2):
            source = slice(g * per_group + m * share, g * per_group + (m + 1) * share)
            ref = blk.at[g, m] if g < 2 else (tok_far, cot_far)[m]
            for chip in range(8):
                first = chip // 4 * (8 * share) + chip % 4 * share
                ref[pl.ds(pl.multiple_of(first + core * (4 * share), 16), share), :] = col[chip, source, :]
                ref[pl.ds(pl.multiple_of(first + (1 - core) * (4 * share), 16), share), :] = col_other[chip, source, :]
    half = out_ref.shape[0] // 2
    for n in range(2):
        part = slice(n * half, (n + 1) * half)
        acc_out = acc_in = 0.0
        for g, bundle in enumerate(bundles):
            tok, cot = (tok_blk[...], cot_blk[...]) if g == 0 else (blk[g - 1, 0], blk[g - 1, 1])
            acc_out += dot(bundle[2 * n * half : (2 * n + 1) * half, :], cot, NT)
            acc_in += dot(tok, bundle[(2 * n + 1) * half : (2 * n + 2) * half, :], NT)
        out_ref[part, :] = acc_out
        in_ref[:, part] = acc_in


def last_kernel(scale, acc_out, acc_in, tok_far, cot_far, far_a, far_b, out_ref, in_ref):
    half = far_a.shape[0] // 2
    for n, bundle in enumerate((far_a, far_b)):
        part = slice(n * half, (n + 1) * half)
        out_ref[part, :] = ((acc_out[part, :] + dot(bundle[:half, :], cot_far[...], NT)) * scale).astype(BF16)
        in_ref[:, part] = ((acc_in[:, part] + dot(tok_far[...], bundle[half:, :], NT)) * scale).astype(BF16)


def plus(a, b):
    return (a.astype(F32) + b.astype(F32)).astype(BF16)


def shards(tokens, cotangent, w_in, w_out, levels):
    z, core, dp = lax.axis_index("z"), lax.axis_index("core"), lax.axis_index("dp")
    pos = jnp.stack([z, core, dp]).astype(jnp.int32)
    w_in, w_out, levels = w_in[0], w_out[0], levels[0]
    d, f = w_in.shape
    t, width = tokens.shape[1:]
    rows = d // 4
    share = rows // 16
    half, cut = f // 2, width // 2
    flops = 2 * t * d * f

    def call(kernel, out_shape, n_scalars, operands, scratch=(), work=0, hbm=(), name=None):
        return pl.pallas_call(
            kernel,
            out_shape=out_shape,
            in_specs=[
                SMEM if n < n_scalars else HBM if n in hbm else VMEM for n in range(len(operands))
            ],
            out_specs=jax.tree.map(lambda _: VMEM, out_shape),
            scratch_shapes=scratch,
            compiler_params=params(),
            cost_estimate=cost(work, work // 256),
            name=name,
        )(*(pltpu.with_memory_space_constraint(x, pltpu.HBM) if n in hbm else x for n, x in enumerate(operands)))

    w_other = shift(w_in, "core", 1)
    tok_ring, cot_ring = [(tokens[0].T,) * 2], [(cotangent[0].T,) * 2]
    for _ in range(3):
        tok_ring.append(both(*tok_ring[-1], "z"))
        cot_ring.append(both(*cot_ring[-1], "z"))
    (tok_l, tok_r), (cot_l, cot_r) = tok_ring[-1], cot_ring[-1]
    far = both(
        jnp.concatenate([tok_l[:cut], cot_l[:cut]]), jnp.concatenate([tok_r[cut:], cot_r[cut:]]), "z"
    )
    far, w_other = lax.optimization_barrier((far, w_other))
    tok_pieces = (tok_ring[0][0], *(p for pair in tok_ring[1:] for p in pair))
    cot_pieces = (cot_ring[0][0], *(p for pair in cot_ring[1:] for p in pair))
    own, *sends = call(
        functools.partial(inputs_kernel, share),
        (sds(2, 8, width, t),) + (sds(2 * share, t),) * 3,
        1,
        (pos, *tok_pieces, *cot_pieces, *far),
        name="inputs",
    )
    other = shift(own, "core", 1)
    shares = shift(sends[0], "dp", 1), shift(sends[2], "dp", -1), shift(sends[1], "dp", 2)
    piece = jnp.concatenate(shares)
    other, piece = lax.optimization_barrier((other, piece))
    size = 256
    hid, bundle, tok_blk, cot_blk = call(
        hidden_kernel,
        (sds(f, t), sds(2 * f, t), sds(rows, t), sds(rows, t)),
        2,
        (pos, levels, own, other, w_in, w_out),
        [
            pltpu.VMEM((d, t), BF16),
            pltpu.VMEM((d, t), BF16),
            pltpu.VMEM((f, t), F32),
            pltpu.VMEM((f // size, d, size), BF16),
            pltpu.VMEM((f // size, size, d), BF16),
            pltpu.SemaphoreType.DMA((2 * f // size,)),
        ],
        hbm=(4, 5),
        name="hidden",
    )

    hid_other = shift(hid, "core", 1)
    bundle_l, bundle_r = both(bundle, bundle, "dp")
    l1, r1 = both(piece, piece, "z")
    terms = call(
        back_kernel,
        sds(8, width, t),
        1,
        (pos, w_in, w_other, hid, hid_other),
        [pltpu.VMEM((8, width, f), BF16), pltpu.SemaphoreType.DMA((8,))],
        2 * flops,
        (1,),
        name="back",
    )
    l1, r1, hid_other = lax.optimization_barrier((l1, r1, hid_other))
    l2, r2 = both(l1, r1, "z")
    l2, r2, terms = lax.optimization_barrier((l2, r2, terms))
    l3, r3 = both(l2, r2, "z")
    part = piece.shape[0] // 2
    far = both(l3[:part], r3[part:], "z")
    right, left = both(terms[4, :cut], terms[4, cut:], "z")
    right, left = lax.optimization_barrier((right, left))
    right, left = both(
        plus(terms[3], jnp.pad(right, ((0, cut), (0, 0)))),
        plus(terms[5], jnp.pad(left, ((cut, 0), (0, 0)))),
        "z",
    )
    right, left, far, bundle_l, bundle_r = lax.optimization_barrier((right, left, far, bundle_l, bundle_r))
    far_a, far_b = both(bundle_l[:f], bundle_r[f:], "dp")
    right, left = both(plus(terms[2], right), plus(terms[6], left), "z")
    right, left = lax.optimization_barrier((right, left))
    right, left = both(plus(terms[1], right), plus(terms[7], left), "z")

    blocks = call(
        blocks_kernel,
        sds(8, *piece.shape),
        1,
        (pos, piece, l1, r1, l2, r2, l3, r3, *far),
        name="blocks",
    )
    blocks_other = shift(blocks, "core", 1)
    scale = 1.0 / math.sqrt(t * lax.axis_size("dp"))

    acc_out, acc_in, tok_far, cot_far = call(
        functools.partial(wgrad_kernel, share),
        (sds(f, rows, dtype=F32), sds(rows, f, dtype=F32), sds(rows, t), sds(rows, t)),
        1,
        (pos, tok_blk, cot_blk, blocks, blocks_other, bundle, bundle_l, bundle_r),
        [pltpu.VMEM((2, 2, rows, t), BF16)],
        flops,
        name="wgrad",
    )
    right, left, acc_out = lax.optimization_barrier((right, left, acc_out))
    input_sum = (terms[0].astype(F32) + right.astype(F32) + left.astype(F32)).astype(BF16)
    grad_out, grad_in = call(
        functools.partial(last_kernel, scale),
        (sds(f, rows), sds(rows, f)),
        0,
        (acc_out, acc_in, tok_far, cot_far, far_a, far_b),
        name="last",
    )
    n_pipe = lax.axis_size("pipe")
    received = lax.ppermute(input_sum, "pipe", [(i, i - 1) for i in range(1, n_pipe)])
    return (received.T[None], grad_in[None], grad_out[None])


def solution(mesh):
    n_pipe, n_dp, n_tensor = mesh.devices.shape
    fine = Mesh(mesh.devices.reshape(n_pipe, n_dp, n_tensor // 2, 2), ("pipe", "dp", "z", "core"))
    tensor = ("z", "core")
    return jax.shard_map(
        shards,
        mesh=fine,
        in_specs=(
            P("pipe", "dp", tensor),
            P("pipe", "dp", tensor),
            P("pipe", None, tensor),
            P("pipe", tensor, None),
            P("pipe", "dp"),
        ),
        out_specs=(P("pipe", "dp", tensor), P("pipe", "dp", tensor), P("pipe", tensor, "dp")),
        check_vma=False,
    )
```
